32 devices in a mesh: groups: 2 (over y), dp: 4 (over x, core), tensor: 4 (over z).
Axes of the slice: x: 2, y: 2, z: 4, core: 2. Of those that a mesh axis runs over, the one named last changes fastest.
Arguments:
- hidden_in: bfloat16 [1024, 8192], P(('groups', 'dp'), 'tensor'), parts along dimension 0, may hold values from -48 to 48
- queries: bfloat16 [1024, 4096], P(('groups', 'dp'), 'tensor'), parts along dimension 0, may hold values from -9 to 9
- keys_values: bfloat16 [1024, 2, 512], P(('groups', 'dp')), parts along dimension 0, may hold values from -6 to 6
- out_weight: bfloat16 [4096, 8192], P('tensor'), may hold values from -0.125 to 0.125
- send_rows: int32 [8, 128], P(('groups', 'dp')), parts along dimension 0, may hold values from 0 to 127, each once within a row
- lengths: int32 [8, 8], P(('groups', 'dp')), parts along dimension 0, may hold values from 1 to 32, 128 in all within a row
- block_scales: bfloat16 [1024, 64], P(('groups', 'dp'), 'tensor'), parts along dimension 0, may hold values from 0.0009994507 to 0.019897461
- value_head: bfloat16 [8192], replicated, may hold values from -0.0625 to 0.0625
Outputs:
- restored: float32 [1024, 8192], P(('groups', 'dp'), 'tensor'), parts along dimension 0
- values: float32 [1024], P(('groups', 'dp')), parts along dimension 0
The draws below stay inside these ranges and needn't reach their ends.
There are 2 independent parts, one for each index of `groups`. The reference program is written for one: setup_inputs(seed, part) draws one part's arguments, and reference() takes and returns one part's arrays. A program takes and returns all parts, laid end to end along the dimension named above; an argument that names none is the same for every part. Nothing has to cross between parts.
Inputs may be any that keep to these rules, and one draw needn't show every extreme that they name: `send_rows`: each row names each of 0 to 127 once. Each dp index's 8 lengths sum to 128; the largest is 32.
All inputs are finite; a program needn't handle non-finite values.
Results may differ from the reference program's by a relative error of at most 0.0085.
Values may be sent and summed in bfloat16 or wider, within the bound.
No kernel may reach another device: no remote copies, remote signals or barrier semaphores. Data moves between devices by JAX's collectives and lax.ppermute only.
A program may use at most 64 MiB of HBM per device.

```python
import math
import jax
import jax.numpy as jnp
import numpy as np
from jax import lax

D = 8192
HEADS = 32
KV_HEADS = 4
HD = 128
BLOCK = 128
TOK_DEV = 128
RESP_DEV = 8
MOST = 32
TOKENS = 512
N_DP = 4
N_TENSOR = 4


def draw_hidden_in(key, part):
    key = jax.random.fold_in(key, 1)
    keys = jax.random.split(key, 3)
    noise = jax.random.truncated_normal(keys[0], -4.0, 4.0, (TOKENS, D), jnp.float32)
    spread = 1.15
    amplitude = 0.4
    base = noise
    row_scale = jnp.exp(jax.random.uniform(keys[1], (TOKENS, 1), jnp.float32, -spread, spread))
    col_scale = jnp.exp(jax.random.uniform(keys[2], (1, D), jnp.float32, -spread, spread))
    return (amplitude * base * row_scale * col_scale).astype(jnp.bfloat16)


def draw_queries(key, part):
    key = jax.random.fold_in(key, 2)
    noise = jax.random.truncated_normal(key, -4.0, 4.0, (TOKENS, HEADS, HD), jnp.float32)
    mixed = noise
    return mixed.reshape(TOKENS, HEADS * HD).astype(jnp.bfloat16)


def draw_keys_values(key, part):
    key = jax.random.fold_in(key, 3)
    noise = jax.random.truncated_normal(key, -4.0, 4.0, (TOKENS, 2, KV_HEADS, HD), jnp.float32)
    stacked = noise
    return stacked.reshape(TOKENS, 2, KV_HEADS * HD).astype(jnp.bfloat16)


def strengthened(values, stream_key, source, target, shards_of, factor):
    def block_of(dim):
        return (jnp.arange(values.shape[dim]) // (values.shape[dim] // shards_of)).reshape((-1,) + (1,) * (values.ndim - 1 - dim))

    one_side = jax.random.permutation(stream_key, shards_of)[block_of(target)]
    far = (block_of(target) + shards_of // 2) % shards_of
    return jnp.where((block_of(source) == one_side) | (block_of(source) == far), factor * values, values)


def block_levels(stream_key, shape, pieces, low, top_value):
    def one(dim, parts):
        heights = jax.random.uniform(jax.random.fold_in(jax.random.fold_in(stream_key, 6), dim), (parts,), jnp.float32, low / len(pieces), top_value / len(pieces))
        return jnp.repeat(jnp.exp(heights), shape[dim] // parts).reshape((-1,) + (1,) * (len(shape) - dim - 1))

    loudness = one(*pieces[0])
    for cut in pieces[1:]:
        loudness = loudness * one(*cut)
    return loudness


def length_profile(count, total, bound, slope):
    loads = [(1 << 20) // math.isqrt(rank ** slope) + 1 for rank in range(2, count + 1)]
    rest, counts = total - bound - (count - 1), [1] * (count - 1)
    while rest > 0:
        movable = [i for i in range(count - 1) if counts[i] < bound]
        mass, budget = sum([loads[i] for i in movable]), rest
        for i in movable:
            extra = min(bound - counts[i], max(1, budget * loads[i] // mass), rest)
            counts[i] = counts[i] + extra
            rest = rest - extra
    return np.array([bound] + counts)


def ragged_sizes(own_key, count, total, limit, skew):
    if count == 2:
        one = jax.random.randint(own_key, (), max(1, total - limit), min(limit, total - 1) + 1)
        return jnp.stack([one, total - one])
    sizes = jnp.asarray(length_profile(count, total, limit, skew), jnp.int32)
    pairs = (count - 1) // 2
    donor, sink = sizes[1:1 + 2 * pairs:2], sizes[2:2 + 2 * pairs:2]
    slack = jnp.minimum(donor - 1, limit - sink)
    moved = jax.random.randint(jax.random.fold_in(own_key, 1), (pairs,), 0, 1 << 20) % (slack + 1)
    sizes = sizes.at[1:1 + 2 * pairs:2].set(donor - moved).at[2:2 + 2 * pairs:2].set(sink + moved)
    return sizes[jax.random.permutation(jax.random.fold_in(own_key, 2), count)]


def centred(own_key, shape, deviation, reach, shards=(), held_as=jnp.bfloat16):
    result = deviation * jax.random.normal(own_key, shape, jnp.float32)
    if shards:
        result = result * block_levels(own_key, shape, shards, -0.22, 0.18)
    return jnp.clip(result, -reach, reach).astype(held_as)


def noise_with(key, extent, scale, reach, shards, heavy, kind=jnp.bfloat16):
    result = scale * jax.random.normal(key, extent, jnp.float32)
    if shards:
        result = result * block_levels(key, extent, shards, -0.22, 0.18)
    return jnp.clip(strengthened(result, jax.random.fold_in(key, 3), *heavy), -reach, reach).astype(kind)


def setup_inputs(seed: int = 0, part: int = 0) -> dict:
    seeds = jax.random.split(jax.random.key(seed), 9)
    part_splits = jax.random.split(jax.random.fold_in(seeds[8], part), 9)
    return {
        "hidden_in": draw_hidden_in(jax.random.fold_in(jax.random.fold_in(seeds[8], part), 71), part),
        "queries": draw_queries(jax.random.fold_in(jax.random.fold_in(seeds[8], part), 71), part),
        "keys_values": draw_keys_values(jax.random.fold_in(jax.random.fold_in(seeds[8], part), 71), part),
        "out_weight": noise_with(seeds[3], (HEADS * HD, D), (HEADS * HD) ** -0.5, 0.125, ((0, 4),), (0, 1, 4, 2.0)),
        "send_rows": jax.vmap(lambda own: jax.random.permutation(own, TOK_DEV))(jax.random.split(part_splits[4], N_DP)).reshape((N_DP, TOK_DEV)).astype(jnp.int32),
        "lengths": jax.vmap(lambda own: ragged_sizes(own, RESP_DEV, TOK_DEV, MOST, 2))(jax.random.split(part_splits[5], N_DP)).reshape((N_DP, RESP_DEV)).astype(jnp.int32),
        "block_scales": jnp.clip(jnp.exp(math.log(0.019897461) - 2.9911416 * jax.random.uniform(part_splits[6], (TOKENS, D // BLOCK), jnp.float32) ** block_levels(part_splits[6], (TOKENS, D // BLOCK), ((0, 4), (1, 4)), -0.2, 0.2)), 0.0009994507, 0.019897461).astype(jnp.bfloat16),
        "value_head": centred(seeds[7], (D,), D ** -0.5, 0.0625),
    }


CLIP_CODE = 448.0
EPS = 1e-06

def balance_index(send_rows):
    per_peer = TOK_DEV // N_DP
    blocks = send_rows.reshape(N_DP, N_DP, per_peer)
    source = jnp.arange(N_DP, dtype=jnp.int32).reshape(N_DP, 1, 1) * TOK_DEV
    arranged = jnp.transpose(blocks + source, (1, 0, 2))
    return arranged.reshape(TOKENS).astype(jnp.int32)

def segment_ids(lengths):
    ends_at = jnp.cumsum(lengths, axis=1)
    position = jnp.arange(TOK_DEV, dtype=jnp.int32)
    return lax.optimization_barrier(jnp.sum((position[None, :, None] >= ends_at[:, None, :]).astype(jnp.int32), axis=2))

def attend(query_rows, key_rows, value_rows, segment):
    scores = jnp.dot(query_rows, key_rows.T, preferred_element_type=jnp.float32) * HD ** (-0.5)
    position = jnp.arange(TOK_DEV, dtype=jnp.int32)
    allowed = (segment[:, None] == segment[None, :]) & (position[:, None] >= position[None, :])
    scores = jnp.where(allowed, scores, -jnp.inf)
    peak_score = lax.optimization_barrier(jnp.max(scores, axis=1, keepdims=True))
    weights = jnp.exp(scores - peak_score)
    weights_low = (weights / lax.optimization_barrier(jnp.sum(weights, axis=1, keepdims=True))).astype(jnp.bfloat16)
    return jnp.dot(weights_low, value_rows, preferred_element_type=jnp.float32).astype(jnp.bfloat16)

def reference(hidden_in, queries, keys_values, out_weight, send_rows, lengths, block_scales, value_head):
    arranged = balance_index(send_rows)
    moved_hidden = jnp.take(hidden_in, arranged, axis=0)
    moved_queries = jnp.take(queries, arranged, axis=0)
    moved_kv = jnp.take(keys_values, arranged, axis=0)
    segments = segment_ids(lengths)
    group_size = HEADS // KV_HEADS

    def per_device(dev_index):
        begin = dev_index * TOK_DEV
        query_dev = lax.dynamic_slice_in_dim(moved_queries, begin, TOK_DEV, 0).reshape(TOK_DEV, HEADS, HD)
        kv_dev = lax.dynamic_slice_in_dim(moved_kv, begin, TOK_DEV, 0).reshape(TOK_DEV, 2, KV_HEADS, HD)
        segment = segments[dev_index]
        outputs = [attend(query_dev[:, head], kv_dev[:, 0, head // group_size], kv_dev[:, 1, head // group_size], segment) for head in range(HEADS)]
        return jnp.concatenate(outputs, axis=1)
    context = lax.map(per_device, jnp.arange(N_DP, dtype=jnp.int32)).reshape(TOKENS, HEADS * HD)
    share_width = HEADS // N_TENSOR * HD

    def add_share(running, dev_index):
        columns = lax.dynamic_slice_in_dim(context, dev_index * share_width, share_width, 1)
        weight_rows = lax.dynamic_slice_in_dim(out_weight, dev_index * share_width, share_width, 0)
        partial_term = jnp.dot(columns, weight_rows, preferred_element_type=jnp.float32).astype(jnp.bfloat16)
        partial_term = lax.optimization_barrier(partial_term)
        return (running + partial_term.astype(jnp.float32), None)
    summed, _ = lax.scan(add_share, jnp.zeros((TOKENS, D), jnp.float32), jnp.arange(N_TENSOR, dtype=jnp.int32))
    residual = moved_hidden.astype(jnp.float32) + summed
    scale_full = jnp.repeat(block_scales.astype(jnp.float32), BLOCK, axis=1)
    code_block = jnp.clip(residual / scale_full, -CLIP_CODE, CLIP_CODE).astype(jnp.bfloat16)
    restored = code_block.astype(jnp.float32) * scale_full
    power_mean = lax.optimization_barrier(jnp.mean(restored * restored, axis=1))
    head_dot = lax.optimization_barrier(jnp.sum(restored * value_head.astype(jnp.float32)[None, :], axis=1))
    values = head_dot / jnp.sqrt(power_mean + EPS)
    return (restored, values)
```

```python
import functools

import jax
import jax.numpy as jnp
from jax import lax
from jax.experimental import pallas as pl
from jax.experimental.pallas import tpu as pltpu
from jax.sharding import PartitionSpec as P

D = 8192
HEADS = 32
KV_HEADS = 4
HD = 128
BLOCK = 128
GROUP = HEADS // KV_HEADS

CLIP_CODE = 448.0
EPS = 1e-06
F32 = jnp.float32
BF16 = jnp.bfloat16
VMEM = pl.BlockSpec(memory_space=pltpu.VMEM)
SMEM = pl.BlockSpec(memory_space=pltpu.SMEM)
ANY = pl.BlockSpec(memory_space=pl.ANY)


def params(mib):
    return pltpu.CompilerParams(vmem_limit_bytes=mib << 20)


def one_hot_columns(send_ref):
    rows = send_ref.shape[1]
    row_id = lax.broadcasted_iota(jnp.int32, (rows, rows), 0)
    return (row_id == send_ref[...]).astype(F32).astype(BF16)


def reorder(one_hot, values):
    return lax.dot_general(
        one_hot, values, (((0,), (0,)), ((), ())), preferred_element_type=F32
    ).astype(BF16)


def pack_qkv_kernel(heads_here, send_ref, q_ref, kv_ref, *refs):
    outs, buf = refs[:-1], refs[-1]
    me = lax.axis_index("dp")
    kv_head = lax.axis_index("tensor") * heads_here // GROUP
    one_hot = one_hot_columns(send_ref)
    width = q_ref.shape[1]
    buf[:, :width] = reorder(one_hot, q_ref[...])
    for pair in range(2):
        start = pl.multiple_of(kv_head * HD, HD)
        part = kv_ref[:, pair, pl.ds(start, HD)]
        buf[:, width + pair * HD : width + (pair + 1) * HD] = reorder(one_hot, part)
    share = outs[0].shape[0]
    for k, out in enumerate(outs):
        start = pl.multiple_of((me ^ k) * share, share)
        out[...] = buf[pl.ds(start, share), :]


def pack_qkv(send_rows, queries, keys_values, n_dp):
    rows, width = queries.shape
    out = jax.ShapeDtypeStruct((rows // n_dp, width + 2 * HD), BF16)
    return pl.pallas_call(
        functools.partial(pack_qkv_kernel, width // HD),
        out_shape=[out] * n_dp,
        in_specs=[VMEM] * 3,
        out_specs=[VMEM] * n_dp,
        scratch_shapes=[pltpu.VMEM((rows, width + 2 * HD), BF16)],
        name="pack_qkv",
    )(send_rows, queries, keys_values)


def pack_hidden_kernel(send_ref, h_ref, *refs):
    outs, buf = refs[:-1], refs[-1]
    me = lax.axis_index("dp")
    buf[...] = reorder(one_hot_columns(send_ref), h_ref[...])
    share = outs[0].shape[0]
    for k, out in enumerate(outs):
        start = pl.multiple_of((me ^ k) * share, share)
        out[...] = buf[pl.ds(start, share), :]


def pack_hidden(send_rows, hidden, n_dp):
    rows, width = hidden.shape
    out = jax.ShapeDtypeStruct((rows // n_dp, width), BF16)
    return pl.pallas_call(
        pack_hidden_kernel,
        out_shape=[out] * n_dp,
        in_specs=[VMEM] * 2,
        out_specs=[VMEM] * n_dp,
        scratch_shapes=[pltpu.VMEM((rows, width), BF16)],
        name="pack_hidden",
    )(send_rows, hidden)


def attend_kernel(len_ref, *refs):
    pieces, out, buf = refs[:-2], refs[-2], refs[-1]
    me = lax.axis_index("dp")
    share = pieces[0].shape[0]
    for k, piece in enumerate(pieces):
        start = pl.multiple_of((me ^ k) * share, share)
        buf[pl.ds(start, share), :] = piece[...]
    rows, width = out.shape
    row_id = lax.broadcasted_iota(jnp.int32, (rows, rows), 0)
    col_id = lax.broadcasted_iota(jnp.int32, (rows, rows), 1)
    row_seg = jnp.zeros((rows, rows), jnp.int32)
    col_seg = jnp.zeros((rows, rows), jnp.int32)
    end = jnp.int32(0)
    for r in range(len_ref.shape[1]):
        end = end + len_ref[0, r]
        row_seg += (row_id >= end).astype(jnp.int32)
        col_seg += (col_id >= end).astype(jnp.int32)
    allowed = (row_seg == col_seg) & (row_id >= col_id)
    keys = buf[:, width : width + HD]
    values = buf[:, width + HD : width + 2 * HD]
    for h in range(width // HD):
        cols = slice(h * HD, (h + 1) * HD)
        scores = lax.dot_general(
            buf[:, cols], keys, (((1,), (1,)), ((), ())), preferred_element_type=F32
        ) * HD ** (-0.5)
        scores = jnp.where(allowed, scores, -jnp.inf)
        peak = jnp.max(scores, axis=1, keepdims=True)
        weights = jnp.exp(scores - peak)
        low = (weights / jnp.sum(weights, axis=1, keepdims=True)).astype(BF16)
        out[:, cols] = jnp.dot(low, values, preferred_element_type=F32).astype(BF16)


def attend(lengths, pieces):
    n_dp = len(pieces)
    share, wide = pieces[0].shape
    rows, width = share * n_dp, wide - 2 * HD
    return pl.pallas_call(
        attend_kernel,
        out_shape=jax.ShapeDtypeStruct((rows, width), BF16),
        in_specs=[SMEM] + [VMEM] * n_dp,
        out_specs=VMEM,
        scratch_shapes=[pltpu.VMEM((rows, wide), BF16)],
        name="attend",
    )(lengths, *pieces)


def step_kernel(n, chunks, step, with_recv, ctx_ref, w_ref, *refs):
    if with_recv:
        recv_r, recv_l, out_r, out_l, w_buf, sem = refs
    else:
        out_r, out_l, w_buf, sem = refs
    width = out_r.shape[1]
    i = lax.axis_index("tensor")
    turn, part = step // chunks, step % chunks
    right = jnp.minimum(n - 1 - turn + i, n - 1) * chunks + part
    left = jnp.maximum(turn - (n - 1 - i), 0) * chunks + part
    copies = []
    for side, block in enumerate((right, left)):
        start = pl.multiple_of(block * width, width)
        copies.append(
            pltpu.make_async_copy(w_ref.at[:, pl.ds(start, width)], w_buf.at[side], sem.at[side])
        )
        copies[-1].start()
    for side, out in enumerate((out_r, out_l)):
        copies[side].wait()
        term = jnp.dot(ctx_ref[...], w_buf[side], preferred_element_type=F32)
        if with_recv:
            term = term + (recv_r, recv_l)[side][...].astype(F32)
        out[...] = term.astype(BF16)


def chain_step(n, chunks, step, context, weight, recv):
    rows, depth = context.shape
    width = weight.shape[1] // (n * chunks)
    out = jax.ShapeDtypeStruct((rows, width), BF16)
    return pl.pallas_call(
        functools.partial(step_kernel, n, chunks, step, recv is not None),
        out_shape=[out] * 2,
        in_specs=[VMEM, ANY] + [VMEM] * (2 if recv is not None else 0),
        out_specs=[VMEM] * 2,
        scratch_shapes=[pltpu.VMEM((2, depth, width), BF16), pltpu.SemaphoreType.DMA((2,))],
        compiler_params=params(16),
        cost_estimate=pl.CostEstimate(
            flops=4 * rows * depth * width, bytes_accessed=4 * depth * width, transcendentals=0
        ),
        name="chain_step",
    )(context, weight, *(recv or ()))


def own_kernel(ctx_ref, w_ref, out, w_buf, sem):
    width = out.shape[1]
    start = pl.multiple_of(lax.axis_index("tensor") * width, width)
    copy = pltpu.make_async_copy(w_ref.at[:, pl.ds(start, width)], w_buf, sem)
    copy.start()
    copy.wait()
    out[...] = jnp.dot(ctx_ref[...], w_buf[...], preferred_element_type=F32)


def own_term(n, context, weight):
    rows, depth = context.shape
    width = weight.shape[1] // n
    return pl.pallas_call(
        own_kernel,
        out_shape=jax.ShapeDtypeStruct((rows, width), F32),
        in_specs=[VMEM, ANY],
        out_specs=VMEM,
        scratch_shapes=[pltpu.VMEM((depth, width), BF16), pltpu.SemaphoreType.DMA],
        compiler_params=params(16),
        cost_estimate=pl.CostEstimate(
            flops=2 * rows * depth * width, bytes_accessed=2 * depth * width, transcendentals=0
        ),
        name="own_term",
    )(context, weight)


def finish_kernel(n_dp, part, width, recv_r, recv_l, own, scale_ref, head_ref, *refs):
    pieces = refs[:n_dp]
    out, sums = refs[-2:]
    earlier = refs[n_dp + 1] if part else None
    me = lax.axis_index("dp")
    i = lax.axis_index("tensor")
    share = pieces[0].shape[0]
    rows, cols = recv_r.shape
    base = part * cols
    for k, piece in enumerate(pieces):
        start = pl.multiple_of((me ^ k) * share, share)
        out[pl.ds(start, share), :] = piece[:, base : base + cols].astype(F32)
    power = jnp.zeros((rows, BLOCK), F32)
    dots = jnp.zeros((rows, BLOCK), F32)
    for b in range(cols // BLOCK):
        here = slice(b * BLOCK, (b + 1) * BLOCK)
        wide = slice(base + b * BLOCK, base + (b + 1) * BLOCK)
        block = base // BLOCK + b
        scale = scale_ref[:, block : block + 1].astype(F32)
        summed = recv_r[:, here].astype(F32) + recv_l[:, here].astype(F32) + own[:, wide]
        residual = out[:, here] + summed
        code = jnp.clip(residual / scale, -CLIP_CODE, CLIP_CODE).astype(BF16)
        restored = code.astype(F32) * scale
        out[:, here] = restored
        power += restored * restored
        start = pl.multiple_of(i * width + base + b * BLOCK, BLOCK)
        dots += restored * head_ref[:, pl.ds(start, BLOCK)].astype(F32)
    total = jnp.concatenate(
        [
            jnp.sum(jnp.transpose(power), axis=0, keepdims=True),
            jnp.sum(jnp.transpose(dots), axis=0, keepdims=True),
            jnp.zeros((6, rows), F32),
        ],
        axis=0,
    )
    if part:
        total = total + earlier[...]
    sums[...] = total


def finish(part, recv_r, recv_l, own, scales, head_row, pieces, before):
    rows, cols = recv_r.shape
    width = own.shape[1]
    n_dp = len(pieces)
    out_spec = pl.BlockSpec((rows, cols), lambda g: (0, part))
    whole = lambda x: pl.BlockSpec(x.shape, lambda g: (0,) * x.ndim)
    args = [recv_r, recv_l, own, scales, head_row, *pieces]
    specs = [whole(x) for x in args]
    aliases = {}
    if before is not None:
        aliases = {len(args): 0}
        args += list(before)
        specs += [ANY, whole(before[1])]
    return pl.pallas_call(
        functools.partial(finish_kernel, n_dp, part, width),
        grid=(1,),
        out_shape=[jax.ShapeDtypeStruct((rows, width), F32), jax.ShapeDtypeStruct((8, rows), F32)],
        in_specs=specs,
        out_specs=[out_spec, pl.BlockSpec((8, rows), lambda g: (0, 0))],
        input_output_aliases=aliases,
        compiler_params=params(32),
        name="finish",
    )(*args)


def exchange(pieces, axis, n):
    return [pieces[0]] + [
        lax.ppermute(pieces[k], axis, [(i, i ^ k) for i in range(n)]) for k in range(1, n)
    ]


def total_over(values, axis, n):
    done = 1
    while done < n:
        radix = min(4, n // done)
        got = [values] + [
            lax.ppermute(values, axis, [(i, i ^ (k * done)) for i in range(n)])
            for k in range(1, radix)
        ]
        values = got[0] + got[1] if radix == 2 else (got[0] + got[1]) + (got[2] + got[3])
        done *= radix
    return values


def per_device(
    n_dp, n, hidden_in, queries, keys_values, out_weight, send_rows, lengths, block_scales, value_head
):
    chunks = 2
    moved = exchange(pack_qkv(send_rows, queries, keys_values, n_dp), "dp", n_dp)
    hidden = exchange(pack_hidden(send_rows, hidden_in, n_dp), "dp", n_dp)
    context = attend(lengths, moved)
    recv = []
    own = None
    for step in range((n - 1) * chunks):
        pair = chain_step(n, chunks, step, context, out_weight, recv[step - chunks] if step >= chunks else None)
        turn = step // chunks
        recv.append(
            (
                lax.ppermute(pair[0], "tensor", [(i, i + 1) for i in range(n - 1) if turn >= i]),
                lax.ppermute(
                    pair[1], "tensor", [(n - 1 - i, n - 2 - i) for i in range(n - 1) if turn >= i]
                ),
            )
        )
    own = own_term(n, context, out_weight)
    head_row = value_head.reshape(1, D)
    result = None
    for part in range(chunks):
        recv_r, recv_l = recv[(n - 2) * chunks + part]
        result = finish(part, recv_r, recv_l, own, block_scales, head_row, hidden, result)
    restored, sums = result
    sums = total_over(sums, "tensor", n)
    values = sums[1] / jnp.sqrt(sums[0] / D + EPS)
    return restored, values


def solution(mesh):
    in_specs = (
        P(("groups", "dp"), "tensor"),
        P(("groups", "dp"), "tensor"),
        P(("groups", "dp"), None, None),
        P("tensor", None),
        P(("groups", "dp"), None),
        P(("groups", "dp"), None),
        P(("groups", "dp"), "tensor"),
        P(),
    )
    out_specs = (P(("groups", "dp"), "tensor"), P(("groups", "dp")))
    return jax.shard_map(
        functools.partial(per_device, mesh.shape["dp"], mesh.shape["tensor"]),
        mesh=mesh,
        in_specs=in_specs,
        out_specs=out_specs,
        check_vma=False,
    )
```

```python
import functools

import jax
import jax.numpy as jnp
from jax import lax
from jax.experimental import pallas as pl
from jax.experimental.pallas import tpu as pltpu
from jax.sharding import PartitionSpec as P

D = 8192
HEADS = 32
KV_HEADS = 4
HD = 128
BLOCK = 128
GROUP = HEADS // KV_HEADS

CLIP_CODE = 448.0
EPS = 1e-06
F32 = jnp.float32
BF16 = jnp.bfloat16
VMEM = pl.BlockSpec(memory_space=pltpu.VMEM)
SMEM = pl.BlockSpec(memory_space=pltpu.SMEM)
ANY = pl.BlockSpec(memory_space=pl.ANY)
HBM = pl.BlockSpec(memory_space=pltpu.HBM)


def params(mib):
    return pltpu.CompilerParams(vmem_limit_bytes=mib << 20)


def one_hot_columns(send_ref):
    rows = send_ref.shape[1]
    row_id = lax.broadcasted_iota(jnp.int32, (rows, rows), 0)
    return (row_id == send_ref[...]).astype(F32).astype(BF16)


def reorder(one_hot, values):
    return lax.dot_general(
        one_hot, values, (((0,), (0,)), ((), ())), preferred_element_type=F32
    ).astype(BF16)


def pack_qkv_kernel(heads_here, send_ref, q_ref, kv_ref, *refs):
    outs, buf = refs[:-1], refs[-1]
    me = lax.axis_index("dp")
    kv_head = lax.axis_index("tensor") * heads_here // GROUP
    one_hot = one_hot_columns(send_ref)
    width = q_ref.shape[1]
    buf[:, :width] = reorder(one_hot, q_ref[...])
    for pair in range(2):
        start = pl.multiple_of(kv_head * HD, HD)
        part = kv_ref[:, pair, pl.ds(start, HD)]
        buf[:, width + pair * HD : width + (pair + 1) * HD] = reorder(one_hot, part)
    share = outs[0].shape[0]
    for k, out in enumerate(outs):
        start = pl.multiple_of((me ^ k) * share, share)
        out[...] = buf[pl.ds(start, share), :]


def pack_qkv(send_rows, queries, keys_values, n_dp):
    rows, width = queries.shape
    out = jax.ShapeDtypeStruct((rows // n_dp, width + 2 * HD), BF16)
    return pl.pallas_call(
        functools.partial(pack_qkv_kernel, width // HD),
        out_shape=[out] * n_dp,
        in_specs=[VMEM] * 3,
        out_specs=[VMEM] * n_dp,
        scratch_shapes=[pltpu.VMEM((rows, width + 2 * HD), BF16)],
        compiler_params=params(63),
        name="pack_qkv",
    )(send_rows, queries, keys_values)


def pack_hidden_kernel(send_ref, h_ref, *refs):
    outs, buf = refs[:-1], refs[-1]
    me = lax.axis_index("dp")
    buf[...] = reorder(one_hot_columns(send_ref), h_ref[...])
    share = outs[0].shape[0]
    for k, out in enumerate(outs):
        start = pl.multiple_of((me ^ k) * share, share)
        out[...] = buf[pl.ds(start, share), :]


def pack_hidden(send_rows, hidden, n_dp):
    rows, width = hidden.shape
    out = jax.ShapeDtypeStruct((rows // n_dp, width), BF16)
    return pl.pallas_call(
        pack_hidden_kernel,
        out_shape=[out] * n_dp,
        in_specs=[VMEM] * 2,
        out_specs=[VMEM] * n_dp,
        scratch_shapes=[pltpu.VMEM((rows, width), BF16)],
        compiler_params=params(4),
        name="pack_hidden",
    )(send_rows, hidden)


def attend_kernel(order, len_ref, *refs):
    n_dp = len(refs) - 6
    pieces, w_ref = refs[:n_dp], refs[n_dp]
    out, first, buf, w_buf, sem = refs[n_dp + 1 :]
    fetch = fetch_block(order, 0, w_ref, w_buf, sem)
    fetch.start()
    me = lax.axis_index("dp")
    share = pieces[0].shape[0]
    for k, piece in enumerate(pieces):
        start = pl.multiple_of((me ^ k) * share, share)
        buf[pl.ds(start, share), :] = piece[...]
    rows, width = out.shape
    row_id = lax.broadcasted_iota(jnp.int32, (rows, rows), 0)
    col_id = lax.broadcasted_iota(jnp.int32, (rows, rows), 1)
    row_seg = jnp.zeros((rows, rows), jnp.int32)
    col_seg = jnp.zeros((rows, rows), jnp.int32)
    end = jnp.int32(0)
    for r in range(len_ref.shape[1]):
        end = end + len_ref[0, r]
        row_seg += (row_id >= end).astype(jnp.int32)
        col_seg += (col_id >= end).astype(jnp.int32)
    allowed = (row_seg == col_seg) & (row_id >= col_id)
    heads = width // HD
    keys = buf[:, width : width + HD]
    values = jnp.concatenate(
        [buf[:, width + HD : width + 2 * HD], jnp.ones((rows, HD), BF16)], axis=1
    )
    query = jnp.concatenate([buf[:, h * HD : (h + 1) * HD] for h in range(heads)], axis=0)
    scores = lax.dot_general(
        query, keys, (((1,), (1,)), ((), ())), preferred_element_type=F32
    ) * HD ** (-0.5)
    scores = jnp.where(allowed[None], scores.reshape(heads, rows, rows), -jnp.inf)
    weights = jnp.exp(scores - jnp.max(scores, axis=2, keepdims=True))
    weights = weights.reshape(heads * rows, rows).astype(BF16)
    mixed = jnp.dot(weights, values, preferred_element_type=F32)
    context = (mixed[:, :HD] / mixed[:, HD:]).astype(BF16)
    context = jnp.concatenate([context[h * rows : (h + 1) * rows] for h in range(heads)], axis=1)
    out[...] = context
    fetch.wait()
    first[...] = jnp.dot(context, w_buf[...], preferred_element_type=F32).astype(BF16)


def fetch_block(order, place, w_ref, w_buf, sem):
    width = w_buf.shape[1]
    start = pl.multiple_of(order(place) * width, width)
    return pltpu.make_async_copy(w_ref.at[:, pl.ds(start, width)], w_buf, sem)


def attend(lengths, pieces, weight, order, cols):
    n_dp = len(pieces)
    share, wide = pieces[0].shape
    rows, width = share * n_dp, wide - 2 * HD
    return pl.pallas_call(
        functools.partial(attend_kernel, order),
        out_shape=[
            jax.ShapeDtypeStruct((rows, width), BF16),
            jax.ShapeDtypeStruct((rows, cols), BF16),
        ],
        in_specs=[SMEM] + [VMEM] * n_dp + [HBM],
        out_specs=[VMEM] * 2,
        scratch_shapes=[
            pltpu.VMEM((rows, wide), BF16),
            pltpu.VMEM((width, cols), BF16),
            pltpu.SemaphoreType.DMA,
        ],
        compiler_params=params(52),
        name="attend",
    )(lengths, *pieces, weight)


def project_kernel(order, ctx_ref, w_ref, *refs):
    count = len(refs) - 2
    outs, w_buf, sems = refs[:count], refs[count], refs[count + 1]
    copies = [
        fetch_block(order, place + 1, w_ref, w_buf.at[place], sems.at[place])
        for place in range(count)
    ]
    for copy in copies:
        copy.start()
    for copy, out, place in zip(copies, outs, range(count)):
        copy.wait()
        term = jnp.dot(ctx_ref[...], w_buf[place], preferred_element_type=F32)
        out[...] = term.astype(out.dtype)


def project(context, weight, order, cols, kept):
    rows, depth = context.shape
    count = weight.shape[1] // cols - 1
    return pl.pallas_call(
        functools.partial(project_kernel, order),
        out_shape=[
            jax.ShapeDtypeStruct((rows, cols), F32 if place >= count - kept else BF16)
            for place in range(count)
        ],
        in_specs=[VMEM, HBM],
        out_specs=[VMEM] * count,
        scratch_shapes=[
            pltpu.VMEM((count, depth, cols), BF16),
            pltpu.SemaphoreType.DMA((count,)),
        ],
        compiler_params=params(52),
        cost_estimate=pl.CostEstimate(
            flops=2 * rows * depth * cols * count,
            bytes_accessed=2 * depth * cols * count,
            transcendentals=0,
        ),
        name="project",
    )(context, weight)


def add_kernel(a_ref, b_ref, out):
    out[...] = (a_ref[...].astype(F32) + b_ref[...].astype(F32)).astype(BF16)


def add(a, b):
    return pl.pallas_call(
        add_kernel,
        out_shape=jax.ShapeDtypeStruct(a.shape, BF16),
        in_specs=[VMEM] * 2,
        out_specs=VMEM,
        compiler_params=params(4),
        name="add",
    )(a, b)


def finish_kernel(n_dp, part, width, recv_r, recv_l, own, scale_ref, head_ref, *refs):
    pieces = refs[:n_dp]
    out, sums = refs[-2:]
    earlier = refs[n_dp + 1] if part else None
    me = lax.axis_index("dp")
    i = lax.axis_index("tensor")
    share = pieces[0].shape[0]
    rows, cols = recv_r.shape
    base = part * cols
    for k, piece in enumerate(pieces):
        start = pl.multiple_of((me ^ k) * share, share)
        out[pl.ds(start, share), :] = piece[:, base : base + cols].astype(F32)
    power = jnp.zeros((rows, BLOCK), F32)
    dots = jnp.zeros((rows, BLOCK), F32)
    for b in range(cols // BLOCK):
        here = slice(b * BLOCK, (b + 1) * BLOCK)
        block = base // BLOCK + b
        scale = scale_ref[:, block : block + 1].astype(F32)
        summed = recv_r[:, here].astype(F32) + recv_l[:, here].astype(F32) + own[:, here]
        residual = out[:, here] + summed
        code = jnp.clip(residual / scale, -CLIP_CODE, CLIP_CODE).astype(BF16)
        restored = code.astype(F32) * scale
        out[:, here] = restored
        power += restored * restored
        start = pl.multiple_of(i * width + base + b * BLOCK, BLOCK)
        dots += restored * head_ref[:, pl.ds(start, BLOCK)].astype(F32)
    total = jnp.concatenate(
        [
            jnp.sum(jnp.transpose(power), axis=0, keepdims=True),
            jnp.sum(jnp.transpose(dots), axis=0, keepdims=True),
            jnp.zeros((6, rows), F32),
        ],
        axis=0,
    )
    if part:
        total = total + earlier[...]
    sums[...] = total


def finish(part, recv_r, recv_l, own, scales, head_row, pieces, before):
    rows, cols = recv_r.shape
    width = pieces[0].shape[1]
    n_dp = len(pieces)
    out_spec = pl.BlockSpec((rows, cols), lambda g: (0, part))
    whole = lambda x: pl.BlockSpec(x.shape, lambda g: (0,) * x.ndim)
    args = [recv_r, recv_l, own, scales, head_row, *pieces]
    specs = [whole(x) for x in args]
    aliases = {}
    if before is not None:
        aliases = {len(args): 0}
        args += list(before)
        specs += [ANY, whole(before[1])]
    return pl.pallas_call(
        functools.partial(finish_kernel, n_dp, part, width),
        grid=(1,),
        out_shape=[jax.ShapeDtypeStruct((rows, width), F32), jax.ShapeDtypeStruct((8, rows), F32)],
        in_specs=specs,
        out_specs=[out_spec, pl.BlockSpec((8, rows), lambda g: (0, 0))],
        input_output_aliases=aliases,
        compiler_params=params(8),
        name="finish",
    )(*args)


def exchange(pieces, axis, n):
    return [pieces[0]] + [
        lax.ppermute(pieces[k], axis, [(i, i ^ k) for i in range(n)]) for k in range(1, n)
    ]


def total_over(values, axis, n):
    done = 1
    while done < n:
        radix = min(4, n // done)
        got = [values] + [
            lax.ppermute(values, axis, [(i, i ^ (k * done)) for i in range(n)])
            for k in range(1, radix)
        ]
        values = got[0] + got[1] if radix == 2 else (got[0] + got[1]) + (got[2] + got[3])
        done *= radix
    return values


def block_order(n, chunks):
    def order(place):
        turn, part = place // chunks, place % chunks
        i = lax.axis_index("tensor")
        low = i < 2
        away = jnp.where(low, 3 - turn, turn)
        if turn < 2:
            shard = away
        elif turn == 2:
            shard = jnp.where(i == 0, 1, jnp.where(i == 1, 0, jnp.where(i == 2, 3, 2)))
        else:
            shard = i
        return shard * chunks + part

    return order if n == 4 else lambda place: jnp.int32(place)


def chain_scatter(terms):
    ends = [(0, 1), (3, 2)]
    pairs = [(0, 1), (1, 0), (2, 3), (3, 2)]
    middle = [(1, 2), (2, 1)]
    move = lambda value, perm: lax.ppermute(value, "tensor", perm)
    outer = [move(terms[0], ends), move(terms[1], ends)]
    inner = []
    for place in range(4):
        inner.append(move(add(terms[place], outer[place]), middle))
        if place < 2:
            outer.append(move(terms[place + 2], ends))
        else:
            outer.append(move(add(terms[place + 2], inner[place - 2]), pairs))
    return [(outer[4 + part], inner[2 + part]) for part in range(2)]


def per_device(
    n_dp, n, hidden_in, queries, keys_values, out_weight, send_rows, lengths, block_scales, value_head
):
    chunks = 2
    cols = hidden_in.shape[1] // chunks
    order = block_order(n, chunks)
    moved = exchange(pack_qkv(send_rows, queries, keys_values, n_dp), "dp", n_dp)
    hidden = exchange(pack_hidden(send_rows, hidden_in, n_dp), "dp", n_dp)
    context, first = attend(lengths, moved, out_weight, order, cols)
    if n == 4:
        rest = project(context, out_weight, order, cols, chunks)
        terms, own = [first, *rest[:-chunks]], rest[-chunks:]
        recv = chain_scatter(terms)
    else:
        partial_term = jnp.dot(context, out_weight, preferred_element_type=F32).astype(BF16)
        summed = lax.psum_scatter(partial_term, "tensor", scatter_dimension=1, tiled=True)
        zero = jnp.zeros((hidden_in.shape[0], cols), BF16)
        recv = [(summed[:, part * cols : (part + 1) * cols], zero) for part in range(chunks)]
        own = [zero] * chunks
    head_row = value_head.reshape(1, D)
    result = None
    for part in range(chunks):
        result = finish(part, *recv[part], own[part], block_scales, head_row, hidden, result)
    restored, sums = result
    sums = total_over(sums, "tensor", n)
    values = sums[1] / jnp.sqrt(sums[0] / D + EPS)
    return restored, values


def solution(mesh):
    in_specs = (
        P(("groups", "dp"), "tensor"),
        P(("groups", "dp"), "tensor"),
        P(("groups", "dp"), None, None),
        P("tensor", None),
        P(("groups", "dp"), None),
        P(("groups", "dp"), None),
        P(("groups", "dp"), "tensor"),
        P(),
    )
    out_specs = (P(("groups", "dp"), "tensor"), P(("groups", "dp")))
    return jax.shard_map(
        functools.partial(per_device, mesh.shape["dp"], mesh.shape["tensor"]),
        mesh=mesh,
        in_specs=in_specs,
        out_specs=out_specs,
        check_vma=False,
    )
```

```python
import functools

import jax
import jax.numpy as jnp
from jax import lax
from jax.experimental import pallas as pl
from jax.experimental.pallas import tpu as pltpu
from jax.sharding import PartitionSpec as P

D = 8192
HEADS = 32
KV_HEADS = 4
HD = 128
BLOCK = 128
GROUP = HEADS // KV_HEADS

CLIP_CODE = 448.0
EPS = 1e-06
F32 = jnp.float32
BF16 = jnp.bfloat16
VMEM = pl.BlockSpec(memory_space=pltpu.VMEM)
SMEM = pl.BlockSpec(memory_space=pltpu.SMEM)
ANY = pl.BlockSpec(memory_space=pl.ANY)
HBM = pl.BlockSpec(memory_space=pltpu.HBM)


def near(shape, dtype=BF16):
    return pltpu.VMEM(shape, dtype)


def held(value):
    return pltpu.with_memory_space_constraint(value, pltpu.VMEM)


def far(value):
    return pltpu.with_memory_space_constraint(value, pltpu.HBM)


def together(*values):
    return lax.optimization_barrier(values)


def params(mib):
    return pltpu.CompilerParams(vmem_limit_bytes=mib << 20)


def one_hot_columns(send_ref):
    rows = send_ref.shape[1]
    row_id = lax.broadcasted_iota(jnp.int32, (rows, rows), 0)
    return (row_id == send_ref[...]).astype(F32).astype(BF16)


def reorder(one_hot, values):
    return lax.dot_general(
        one_hot, values, (((0,), (0,)), ((), ())), preferred_element_type=F32
    ).astype(BF16)


def pack_qkv_kernel(heads_here, send_ref, q_ref, kv_ref, *refs):
    outs, buf = refs[:-1], refs[-1]
    me = lax.axis_index("dp")
    kv_head = lax.axis_index("tensor") * heads_here // GROUP
    one_hot = one_hot_columns(send_ref)
    width = q_ref.shape[1]
    buf[:, :width] = reorder(one_hot, q_ref[...])
    for pair in range(2):
        start = pl.multiple_of(kv_head * HD, HD)
        part = kv_ref[:, pair, pl.ds(start, HD)]
        buf[:, width + pair * HD : width + (pair + 1) * HD] = reorder(one_hot, part)
    share = outs[0].shape[0]
    for k, out in enumerate(outs):
        start = pl.multiple_of((me ^ k) * share, share)
        out[...] = buf[pl.ds(start, share), :]


def pack_qkv(send_rows, queries, keys_values, n_dp):
    rows, width = queries.shape
    out = near((rows // n_dp, width + 2 * HD))
    return pl.pallas_call(
        functools.partial(pack_qkv_kernel, width // HD),
        out_shape=[out] * n_dp,
        in_specs=[VMEM] * 3,
        out_specs=[VMEM] * n_dp,
        scratch_shapes=[pltpu.VMEM((rows, width + 2 * HD), BF16)],
        compiler_params=params(8),
        name="pack_qkv",
    )(far(send_rows), far(queries), far(keys_values))


FETCHES = 4


class Fetch:
    def __init__(self, order, place, w_ref, out, sems):
        depth, width = out.shape
        start = pl.multiple_of(order(place) * width, width)
        share = depth // FETCHES
        self.copies = []
        for k in range(FETCHES):
            rows = pl.ds(k * share, share)
            self.copies.append(
                pltpu.make_async_copy(w_ref.at[rows, pl.ds(start, width)], out.at[rows, :], sems.at[k])
            )
            self.copies[-1].start()

    def wait(self):
        for copy in self.copies:
            copy.wait()


def fetch_sems(blocks):
    return pltpu.SemaphoreType.DMA((max(blocks, 1), FETCHES))


def pack_hidden_kernel(n_dp, order, send_ref, h_ref, w_ref, *refs):
    outs, blocks, (buf, sems) = refs[:n_dp], refs[n_dp:-2], refs[-2:]
    copies = [Fetch(order, k, w_ref, block, sems.at[k]) for k, block in enumerate(blocks)]
    me = lax.axis_index("dp")
    buf[...] = reorder(one_hot_columns(send_ref), h_ref[...])
    share = outs[0].shape[0]
    for k, out in enumerate(outs):
        start = pl.multiple_of((me ^ k) * share, share)
        out[...] = buf[pl.ds(start, share), :]
    for copy in copies:
        copy.wait()


def pack_hidden(send_rows, hidden, weight, n_dp, order, cols, blocks):
    rows, width = hidden.shape
    depth = weight.shape[0]
    got = pl.pallas_call(
        functools.partial(pack_hidden_kernel, n_dp, order),
        out_shape=[near((rows // n_dp, width))] * n_dp + [near((depth, cols))] * blocks,
        in_specs=[VMEM] * 2 + [HBM],
        out_specs=[VMEM] * (n_dp + blocks),
        scratch_shapes=[pltpu.VMEM((rows, width), BF16), fetch_sems(blocks)],
        compiler_params=params(4 + 2 * blocks),
        name="pack_hidden",
    )(far(send_rows), far(hidden), far(weight))
    return got[:n_dp], got[n_dp:]


def attend_kernel(n_dp, len_ref, *refs):
    pieces, refs = refs[:n_dp], refs[n_dp:]
    w_ref, out, first, buf = refs if len(refs) == 4 else (None, refs[0], None, refs[1])
    me = lax.axis_index("dp")
    share = pieces[0].shape[0]
    for k, piece in enumerate(pieces):
        start = pl.multiple_of((me ^ k) * share, share)
        buf[pl.ds(start, share), :] = piece[...]
    rows, width = out.shape
    row_id = lax.broadcasted_iota(jnp.int32, (rows, rows), 0)
    col_id = lax.broadcasted_iota(jnp.int32, (rows, rows), 1)
    row_seg = jnp.zeros((rows, rows), jnp.int32)
    col_seg = jnp.zeros((rows, rows), jnp.int32)
    end = jnp.int32(0)
    for r in range(len_ref.shape[1]):
        end = end + len_ref[0, r]
        row_seg += (row_id >= end).astype(jnp.int32)
        col_seg += (col_id >= end).astype(jnp.int32)
    allowed = (row_seg == col_seg) & (row_id >= col_id)
    heads = width // HD
    keys = buf[:, width : width + HD]
    values = jnp.concatenate(
        [buf[:, width + HD : width + 2 * HD], jnp.ones((rows, HD), BF16)], axis=1
    )
    query = jnp.concatenate([buf[:, h * HD : (h + 1) * HD] for h in range(heads)], axis=0)
    scores = lax.dot_general(
        query, keys, (((1,), (1,)), ((), ())), preferred_element_type=F32
    ) * HD ** (-0.5)
    scores = jnp.where(allowed[None], scores.reshape(heads, rows, rows), -jnp.inf)
    weights = jnp.exp(scores - jnp.max(scores, axis=2, keepdims=True))
    weights = weights.reshape(heads * rows, rows).astype(BF16)
    mixed = jnp.dot(weights, values, preferred_element_type=F32)
    context = (mixed[:, :HD] / mixed[:, HD:]).astype(BF16)
    context = jnp.concatenate([context[h * rows : (h + 1) * rows] for h in range(heads)], axis=1)
    out[...] = context
    if first is not None:
        first[...] = jnp.dot(context, w_ref[...], preferred_element_type=F32).astype(BF16)


def attend(lengths, pieces, block=None):
    n_dp = len(pieces)
    share, wide = pieces[0].shape
    rows, width = share * n_dp, wide - 2 * HD
    args = [lengths, *map(held, pieces)]
    outs = [near((rows, width))]
    if block is not None:
        args.append(held(block))
        outs.append(near((rows, block.shape[1])))
    return pl.pallas_call(
        functools.partial(attend_kernel, n_dp),
        out_shape=outs,
        in_specs=[SMEM] + [VMEM] * (len(args) - 1),
        out_specs=[VMEM] * len(outs),
        scratch_shapes=[pltpu.VMEM((rows, wide), BF16)],
        compiler_params=params(8),
        name="attend",
    )(*args)


def project_kernel(order, at, ctx_ref, w_ref, *outs):
    for k, out in enumerate(outs):
        width = out.shape[1]
        start = pl.multiple_of(order(at + k) * width, width)
        term = jnp.dot(ctx_ref[...], w_ref[:, pl.ds(start, width)], preferred_element_type=F32)
        out[...] = term.astype(out.dtype)


def project(context, weight, order, at, cols, kept):
    rows, depth = context.shape
    count = weight.shape[1] // cols - at
    return pl.pallas_call(
        functools.partial(project_kernel, order, at),
        out_shape=[
            near((rows, cols), F32 if place >= count - kept else BF16) for place in range(count)
        ],
        in_specs=[VMEM] * 2,
        out_specs=[VMEM] * count,
        compiler_params=params(8),
        cost_estimate=pl.CostEstimate(
            flops=2 * rows * depth * cols * count,
            bytes_accessed=2 * depth * cols * count,
            transcendentals=0,
        ),
        name="project",
    )(held(context), held(weight))


def add_kernel(count, *refs):
    for a_ref, b_ref, out in zip(refs[:count], refs[count : 2 * count], refs[-count:]):
        out[...] = (a_ref[...].astype(F32) + b_ref[...].astype(F32)).astype(BF16)


def add(*pairs, after=()):
    count = len(pairs)
    left, right = zip(*pairs)
    return pl.pallas_call(
        functools.partial(add_kernel, count),
        out_shape=[near(a.shape) for a in (*after, *left)],
        in_specs=[VMEM] * (2 * count) + [ANY] * len(after),
        out_specs=[ANY] * len(after) + [VMEM] * count,
        input_output_aliases={2 * count + k: k for k in range(len(after))},
        compiler_params=params(4),
        name="add",
    )(*map(held, left), *map(held, right), *map(held, after))


def finish_kernel(n_dp, part, width, recv_r, recv_l, own, scale_ref, head_ref, *refs):
    pieces = refs[:n_dp]
    restored_ref, sums, out, sem = refs[-4:]
    earlier = refs[n_dp + 1] if part else None
    me = lax.axis_index("dp")
    i = lax.axis_index("tensor")
    share = pieces[0].shape[0]
    rows, cols = recv_r.shape
    base = part * cols
    for k, piece in enumerate(pieces):
        start = pl.multiple_of((me ^ k) * share, share)
        out[pl.ds(start, share), :] = piece[:, base : base + cols].astype(F32)
    power = jnp.zeros((rows, BLOCK), F32)
    dots = jnp.zeros((rows, BLOCK), F32)
    for b in range(cols // BLOCK):
        here = slice(b * BLOCK, (b + 1) * BLOCK)
        block = base // BLOCK + b
        scale = scale_ref[:, block : block + 1].astype(F32)
        summed = recv_r[:, here].astype(F32) + recv_l[:, here].astype(F32) + own[:, here]
        residual = out[:, here] + summed
        code = jnp.clip(residual / scale, -CLIP_CODE, CLIP_CODE).astype(BF16)
        restored = code.astype(F32) * scale
        out[:, here] = restored
        power += restored * restored
        start = pl.multiple_of(i * width + base + b * BLOCK, BLOCK)
        dots += restored * head_ref[:, pl.ds(start, BLOCK)].astype(F32)
    copy = pltpu.make_async_copy(out, restored_ref.at[:, pl.ds(base, cols)], sem)
    copy.start()
    total = jnp.concatenate(
        [
            jnp.sum(jnp.transpose(power), axis=0, keepdims=True),
            jnp.sum(jnp.transpose(dots), axis=0, keepdims=True),
            jnp.zeros((6, rows), F32),
        ],
        axis=0,
    )
    if part:
        total = total + earlier[...]
    sums[...] = total
    copy.wait()


def finish(part, recv_r, recv_l, own, scales, head_row, pieces, before):
    rows, cols = recv_r.shape
    width = pieces[0].shape[1]
    n_dp = len(pieces)
    args = [*map(held, (recv_r, recv_l, own)), scales, head_row, *map(held, pieces)]
    specs = [VMEM] * len(args)
    aliases = {}
    if before is not None:
        aliases = {len(args): 0}
        args += [before[0], held(before[1])]
        specs += [ANY, VMEM]
    return pl.pallas_call(
        functools.partial(finish_kernel, n_dp, part, width),
        out_shape=[jax.ShapeDtypeStruct((rows, width), F32), jax.ShapeDtypeStruct((8, rows), F32)],
        in_specs=specs,
        out_specs=[ANY, VMEM],
        input_output_aliases=aliases,
        scratch_shapes=[pltpu.VMEM((rows, cols), F32), pltpu.SemaphoreType.DMA],
        compiler_params=params(8),
        name="finish",
    )(*args)


def swap(piece, axis, n, bits):
    return lax.ppermute(piece, axis, [(i, i ^ bits) for i in range(n)])


def exchange(pieces, axis, n):
    return [pieces[0]] + [swap(pieces[k], axis, n, k) for k in range(1, n)]


def total_over(values, axis, n):
    done = 1
    while done < n:
        radix = min(4, n // done)
        got = [values] + [swap(values, axis, n, k * done) for k in range(1, radix)]
        values = got[0] + got[1] if radix == 2 else (got[0] + got[1]) + (got[2] + got[3])
        done *= radix
    return values


def block_order(n, chunks):
    def order(place):
        turn, part = place // chunks, place % chunks
        i = lax.axis_index("tensor")
        low = i < 2
        away = jnp.where(low, 3 - turn, turn)
        if turn < 2:
            shard = away
        elif turn == 2:
            shard = jnp.where(i == 0, 1, jnp.where(i == 1, 0, jnp.where(i == 2, 3, 2)))
        else:
            shard = i
        return shard * chunks + part

    return order if n == 4 else lambda place: jnp.int32(place)


def chain_scatter(terms, beside):
    ends = [(0, 1), (3, 2)]
    pairs = [(0, 1), (1, 0), (2, 3), (3, 2)]
    middle = [(1, 2), (2, 1)]
    move = lambda value, perm: lax.ppermute(value, "tensor", perm)
    t = list(terms)
    outer = [move(t[0], ends), move(t[1], ends)]
    t[2], t[3], sent = add((t[0], outer[0]), after=[t[2], t[3]])
    outer.append(move(t[2], ends))
    inner = [move(sent, middle)]
    t[3], t[4], *beside, sent = add((t[1], outer[1]), after=[t[3], t[4], *beside])
    outer.append(move(t[3], ends))
    inner.append(move(sent, middle))
    t[5], sent, owed = add((t[2], outer[2]), (t[4], inner[0]), after=[t[5]])
    outer.append(move(owed, pairs))
    inner.append(move(sent, middle))
    sent, owed = add((t[3], outer[3]), (t[5], inner[1]))
    outer.append(move(owed, pairs))
    inner.append(move(sent, middle))
    return [(outer[4 + part], inner[2 + part]) for part in range(2)], beside


def per_device(
    n_dp, n, hidden_in, queries, keys_values, out_weight, send_rows, lengths, block_scales, value_head
):
    chunks = 2
    cols = hidden_in.shape[1] // chunks
    order = block_order(n, chunks)
    packed = pack_qkv(send_rows, queries, keys_values, n_dp)
    *packed, hidden_in = together(*packed, hidden_in)
    moved = exchange(packed, "dp", n_dp)
    packed_hidden, w_early = pack_hidden(
        send_rows, hidden_in, out_weight, n_dp, order, cols, 1 if n == 4 else 0
    )
    hidden = exchange(packed_hidden, "dp", n_dp)
    if n == 4:
        context, first = attend(lengths, moved, w_early[0])
        rest = project(context, out_weight, order, 1, cols, chunks)
        terms, own = [first, *rest[:-chunks]], rest[-chunks:]
        recv, hidden[1:] = chain_scatter(terms, hidden[1:])
    else:
        context = attend(lengths, moved)[0]
        partial_term = jnp.dot(context, out_weight, preferred_element_type=F32).astype(BF16)
        summed = lax.psum_scatter(partial_term, "tensor", scatter_dimension=1, tiled=True)
        zero = jnp.zeros((hidden_in.shape[0], cols), BF16)
        recv = [(summed[:, part * cols : (part + 1) * cols], zero) for part in range(chunks)]
        own = [zero] * chunks
    head_row = value_head.reshape(1, D)
    result = None
    for part in range(chunks):
        result = finish(part, *recv[part], own[part], block_scales, head_row, hidden, result)
    restored, sums = result
    sums = total_over(sums, "tensor", n)
    values = sums[1] / jnp.sqrt(sums[0] / D + EPS)
    return restored, values


def solution(mesh):
    in_specs = (
        P(("groups", "dp"), "tensor"),
        P(("groups", "dp"), "tensor"),
        P(("groups", "dp"), None, None),
        P("tensor", None),
        P(("groups", "dp"), None),
        P(("groups", "dp"), None),
        P(("groups", "dp"), "tensor"),
        P(),
    )
    out_specs = (P(("groups", "dp"), "tensor"), P(("groups", "dp")))
    return jax.shard_map(
        functools.partial(per_device, mesh.shape["dp"], mesh.shape["tensor"]),
        mesh=mesh,
        in_specs=in_specs,
        out_specs=out_specs,
        check_vma=False,
    )
```

```python
import functools

import jax
import jax.numpy as jnp
from jax import lax
from jax.experimental import pallas as pl
from jax.experimental.pallas import tpu as pltpu
from jax.sharding import PartitionSpec as P

D = 8192
HEADS = 32
KV_HEADS = 4
HD = 128
BLOCK = 128
GROUP = HEADS // KV_HEADS

CLIP_CODE = 448.0
EPS = 1e-06
F32 = jnp.float32
BF16 = jnp.bfloat16
VMEM = pl.BlockSpec(memory_space=pltpu.VMEM)
SMEM = pl.BlockSpec(memory_space=pltpu.SMEM)
ANY = pl.BlockSpec(memory_space=pl.ANY)
HBM = pl.BlockSpec(memory_space=pltpu.HBM)


def near(shape, dtype=BF16):
    return pltpu.VMEM(shape, dtype)


def held(value):
    return pltpu.with_memory_space_constraint(value, pltpu.VMEM)


def far(value):
    return pltpu.with_memory_space_constraint(value, pltpu.HBM)


def together(*values):
    return lax.optimization_barrier(values)


def params(mib):
    return pltpu.CompilerParams(vmem_limit_bytes=mib << 20)


def one_hot_columns(send_ref):
    rows = send_ref.shape[1]
    row_id = lax.broadcasted_iota(jnp.int32, (rows, rows), 0)
    return (row_id == send_ref[...]).astype(F32).astype(BF16)


def reorder(one_hot, values):
    return lax.dot_general(
        one_hot, values, (((0,), (0,)), ((), ())), preferred_element_type=F32
    ).astype(BF16)


def pack_qkv_kernel(heads_here, send_ref, q_ref, kv_ref, *refs):
    outs, buf = refs[:-1], refs[-1]
    me = lax.axis_index("dp")
    kv_head = lax.axis_index("tensor") * heads_here // GROUP
    one_hot = one_hot_columns(send_ref)
    width = q_ref.shape[1]
    buf[:, :width] = reorder(one_hot, q_ref[...])
    for pair in range(2):
        start = pl.multiple_of(kv_head * HD, HD)
        part = kv_ref[:, pair, pl.ds(start, HD)]
        buf[:, width + pair * HD : width + (pair + 1) * HD] = reorder(one_hot, part)
    share = outs[0].shape[0]
    for k, out in enumerate(outs):
        start = pl.multiple_of((me ^ k) * share, share)
        out[...] = buf[pl.ds(start, share), :]


def pack_qkv(send_rows, queries, keys_values, n_dp):
    rows, width = queries.shape
    out = near((rows // n_dp, width + 2 * HD))
    return pl.pallas_call(
        functools.partial(pack_qkv_kernel, width // HD),
        out_shape=[out] * n_dp,
        in_specs=[VMEM] * 3,
        out_specs=[VMEM] * n_dp,
        scratch_shapes=[pltpu.VMEM((rows, width + 2 * HD), BF16)],
        compiler_params=params(8),
        name="pack_qkv",
    )(far(send_rows), far(queries), far(keys_values))


FETCHES = 4


class Fetch:
    def __init__(self, order, place, w_ref, out, sems):
        depth, width = out.shape
        start = pl.multiple_of(order(place) * width, width)
        share = depth // FETCHES
        self.copies = []
        for k in range(FETCHES):
            rows = pl.ds(k * share, share)
            self.copies.append(
                pltpu.make_async_copy(w_ref.at[rows, pl.ds(start, width)], out.at[rows, :], sems.at[k])
            )
            self.copies[-1].start()

    def wait(self):
        for copy in self.copies:
            copy.wait()


def fetch_sems(blocks):
    return pltpu.SemaphoreType.DMA((max(blocks, 1), FETCHES))


def pack_hidden_kernel(n_dp, order, send_ref, h_ref, w_ref, *refs):
    outs, blocks, (buf, sems) = refs[:n_dp], refs[n_dp:-2], refs[-2:]
    copies = [Fetch(order, k, w_ref, block, sems.at[k]) for k, block in enumerate(blocks)]
    me = lax.axis_index("dp")
    buf[...] = reorder(one_hot_columns(send_ref), h_ref[...])
    share = outs[0].shape[0]
    for k, out in enumerate(outs):
        start = pl.multiple_of((me ^ k) * share, share)
        out[...] = buf[pl.ds(start, share), :]
    for copy in copies:
        copy.wait()


def pack_hidden(send_rows, hidden, weight, n_dp, order, cols, blocks):
    rows, width = hidden.shape
    depth = weight.shape[0]
    got = pl.pallas_call(
        functools.partial(pack_hidden_kernel, n_dp, order),
        out_shape=[near((rows // n_dp, width))] * n_dp + [near((depth, cols))] * blocks,
        in_specs=[VMEM] * 2 + [HBM],
        out_specs=[VMEM] * (n_dp + blocks),
        scratch_shapes=[pltpu.VMEM((rows, width), BF16), fetch_sems(blocks)],
        compiler_params=params(4 + 2 * blocks),
        name="pack_hidden",
    )(far(send_rows), far(hidden), far(weight))
    return got[:n_dp], got[n_dp:]


def attend_kernel(n_dp, len_ref, *refs):
    pieces, refs = refs[:n_dp], refs[n_dp:]
    w_ref, out, first, buf = refs if len(refs) == 4 else (None, refs[0], None, refs[1])
    me = lax.axis_index("dp")
    share = pieces[0].shape[0]
    for k, piece in zip(arrivals(n_dp), pieces):
        start = pl.multiple_of((me ^ k) * share, share)
        buf[pl.ds(start, share), :] = piece[...]
    rows, width = out.shape
    row_id = lax.broadcasted_iota(jnp.int32, (rows, rows), 0)
    col_id = lax.broadcasted_iota(jnp.int32, (rows, rows), 1)
    row_seg = jnp.zeros((rows, rows), jnp.int32)
    col_seg = jnp.zeros((rows, rows), jnp.int32)
    end = jnp.int32(0)
    for r in range(len_ref.shape[1]):
        end = end + len_ref[0, r]
        row_seg += (row_id >= end).astype(jnp.int32)
        col_seg += (col_id >= end).astype(jnp.int32)
    allowed = (row_seg == col_seg) & (row_id >= col_id)
    heads = width // HD
    keys = buf[:, width : width + HD]
    values = jnp.concatenate(
        [buf[:, width + HD : width + 2 * HD], jnp.ones((rows, HD), BF16)], axis=1
    )
    query = jnp.concatenate([buf[:, h * HD : (h + 1) * HD] for h in range(heads)], axis=0)
    scores = lax.dot_general(
        query, keys, (((1,), (1,)), ((), ())), preferred_element_type=F32
    ) * HD ** (-0.5)
    scores = jnp.where(allowed[None], scores.reshape(heads, rows, rows), -jnp.inf)
    weights = jnp.exp(scores - jnp.max(scores, axis=2, keepdims=True))
    weights = weights.reshape(heads * rows, rows).astype(BF16)
    mixed = jnp.dot(weights, values, preferred_element_type=F32)
    context = (mixed[:, :HD] / mixed[:, HD:]).astype(BF16)
    context = jnp.concatenate([context[h * rows : (h + 1) * rows] for h in range(heads)], axis=1)
    out[...] = context
    if first is not None:
        first[...] = jnp.dot(context, w_ref[...], preferred_element_type=F32).astype(BF16)


def arrivals(n_dp):
    return [0, 2, 1, *range(3, n_dp)] if n_dp > 2 else [*range(n_dp)]


def attend(lengths, pieces, block=None):
    n_dp = len(pieces)
    share, wide = pieces[0].shape
    rows, width = share * n_dp, wide - 2 * HD
    args = [lengths, *(held(pieces[k]) for k in arrivals(n_dp))]
    outs = [near((rows, width))]
    if block is not None:
        args.append(held(block))
        outs.append(near((rows, block.shape[1])))
    return pl.pallas_call(
        functools.partial(attend_kernel, n_dp),
        out_shape=outs,
        in_specs=[SMEM] + [VMEM] * (len(args) - 1),
        out_specs=[VMEM] * len(outs),
        scratch_shapes=[pltpu.VMEM((rows, wide), BF16)],
        compiler_params=params(8),
        name="attend",
    )(*args)


def project_kernel(order, at, ctx_ref, w_ref, *outs):
    for k, out in enumerate(outs):
        width = out.shape[1]
        start = pl.multiple_of(order(at + k) * width, width)
        term = jnp.dot(ctx_ref[...], w_ref[:, pl.ds(start, width)], preferred_element_type=F32)
        out[...] = term.astype(out.dtype)


def project(context, weight, order, at, cols, kept):
    rows, depth = context.shape
    count = weight.shape[1] // cols - at
    return pl.pallas_call(
        functools.partial(project_kernel, order, at),
        out_shape=[
            near((rows, cols), F32 if place >= count - kept else BF16) for place in range(count)
        ],
        in_specs=[VMEM] * 2,
        out_specs=[VMEM] * count,
        compiler_params=params(8),
        cost_estimate=pl.CostEstimate(
            flops=2 * rows * depth * cols * count,
            bytes_accessed=2 * depth * cols * count,
            transcendentals=0,
        ),
        name="project",
    )(held(context), held(weight))


def add_kernel(count, *refs):
    for a_ref, b_ref, out in zip(refs[:count], refs[count : 2 * count], refs[-count:]):
        out[...] = (a_ref[...].astype(F32) + b_ref[...].astype(F32)).astype(BF16)


def add(*pairs, after=()):
    count = len(pairs)
    left, right = zip(*pairs)
    return pl.pallas_call(
        functools.partial(add_kernel, count),
        out_shape=[near(a.shape) for a in (*after, *left)],
        in_specs=[VMEM] * (2 * count) + [ANY] * len(after),
        out_specs=[ANY] * len(after) + [VMEM] * count,
        input_output_aliases={2 * count + k: k for k in range(len(after))},
        compiler_params=params(4),
        name="add",
    )(*map(held, left), *map(held, right), *map(held, after))


def finish_kernel(n_dp, part, width, recv_r, recv_l, own, scale_ref, head_ref, *refs):
    pieces = refs[:n_dp]
    out, sums = refs[-2:]
    earlier = refs[n_dp] if part else None
    me = lax.axis_index("dp")
    i = lax.axis_index("tensor")
    share = pieces[0].shape[0]
    rows, cols = recv_r.shape
    base = part * cols
    for k, piece in enumerate(pieces):
        start = pl.multiple_of((me ^ k) * share, share)
        out[pl.ds(start, share), :] = piece[:, base : base + cols].astype(F32)
    power = jnp.zeros((rows, BLOCK), F32)
    dots = jnp.zeros((rows, BLOCK), F32)
    for b in range(cols // BLOCK):
        here = slice(b * BLOCK, (b + 1) * BLOCK)
        block = base // BLOCK + b
        scale = scale_ref[:, block : block + 1].astype(F32)
        summed = recv_r[:, here].astype(F32) + recv_l[:, here].astype(F32) + own[:, here]
        residual = out[:, here] + summed
        code = jnp.clip(residual / scale, -CLIP_CODE, CLIP_CODE).astype(BF16)
        restored = code.astype(F32) * scale
        out[:, here] = restored
        power += restored * restored
        start = pl.multiple_of(i * width + base + b * BLOCK, BLOCK)
        dots += restored * head_ref[:, pl.ds(start, BLOCK)].astype(F32)
    total = jnp.concatenate(
        [
            jnp.sum(jnp.transpose(power), axis=0, keepdims=True),
            jnp.sum(jnp.transpose(dots), axis=0, keepdims=True),
            jnp.zeros((6, rows), F32),
        ],
        axis=0,
    )
    if part:
        total = total + earlier[...]
    sums[...] = total


def finish(part, recv_r, recv_l, own, scales, head_row, pieces, earlier=None, stored=None):
    rows, cols = recv_r.shape
    width = pieces[0].shape[1]
    n_dp = len(pieces)
    args = [*map(held, (recv_r, recv_l, own)), scales, head_row, *map(held, pieces)]
    outs = [near((rows, cols), F32), near((8, rows), F32)]
    if part:
        args += [held(earlier), far(stored)]
        outs = [jax.ShapeDtypeStruct(stored.shape, F32), *outs]
    return pl.pallas_call(
        functools.partial(finish_kernel, n_dp, part, width),
        out_shape=outs,
        in_specs=[VMEM] * (len(args) - 1) + [ANY if part else VMEM],
        out_specs=[ANY] * (len(outs) - 2) + [VMEM] * 2,
        input_output_aliases={len(args) - 1: 0} if part else {},
        compiler_params=params(8),
        name="finish",
    )(*args)


def store_kernel(part, value_ref, *refs):
    out, sem = refs[-2:]
    cols = value_ref.shape[1]
    copy = pltpu.make_async_copy(value_ref, out.at[:, pl.ds(part * cols, cols)], sem)
    copy.start()
    copy.wait()


def store(part, chunks, value, before):
    rows, cols = value.shape
    args = [held(value)] + ([] if before is None else [before])
    return pl.pallas_call(
        functools.partial(store_kernel, part),
        out_shape=jax.ShapeDtypeStruct((rows, cols * chunks), F32),
        in_specs=[VMEM] + [ANY] * (len(args) - 1),
        out_specs=ANY,
        input_output_aliases={1: 0} if len(args) > 1 else {},
        scratch_shapes=[pltpu.SemaphoreType.DMA],
        compiler_params=params(4),
        cost_estimate=pl.CostEstimate(
            flops=0, bytes_accessed=4 * rows * cols, transcendentals=0
        ),
        name="store",
    )(*args)


def swap(piece, axis, n, bits):
    return lax.ppermute(piece, axis, [(i, i ^ bits) for i in range(n)])


def exchange(pieces, axis, n):
    return [pieces[0]] + [swap(pieces[k], axis, n, k) for k in range(1, n)]


def total_over(values, axis, n):
    done = 1
    while done < n:
        radix = min(4, n // done)
        got = [values] + [swap(values, axis, n, k * done) for k in range(1, radix)]
        values = got[0] + got[1] if radix == 2 else (got[2] + got[0]) + (got[1] + got[3])
        done *= radix
    return values


def block_order(n, chunks):
    def order(place):
        turn, part = place // chunks, place % chunks
        i = lax.axis_index("tensor")
        low = i < 2
        away = jnp.where(low, 3 - turn, turn)
        if turn < 2:
            shard = away
        elif turn == 2:
            shard = jnp.where(i == 0, 1, jnp.where(i == 1, 0, jnp.where(i == 2, 3, 2)))
        else:
            shard = i
        return shard * chunks + part

    return order if n == 4 else lambda place: jnp.int32(place)


def chain_scatter(terms, beside):
    ends = [(0, 1), (3, 2)]
    pairs = [(0, 1), (1, 0), (2, 3), (3, 2)]
    middle = [(1, 2), (2, 1)]
    move = lambda value, perm: lax.ppermute(value, "tensor", perm)
    t = list(terms)
    outer = [move(t[0], ends), move(t[1], ends)]
    t[2], t[3], sent = add((t[0], outer[0]), after=[t[2], t[3]])
    outer.append(move(t[2], ends))
    inner = [move(sent, middle)]
    t[3], t[4], *beside, sent = add((t[1], outer[1]), after=[t[3], t[4], *beside])
    outer.append(move(t[3], ends))
    inner.append(move(sent, middle))
    t[5], sent, owed = add((t[2], outer[2]), (t[4], inner[0]), after=[t[5]])
    outer.append(move(owed, pairs))
    inner.append(move(sent, middle))
    sent, owed = add((t[3], outer[3]), (t[5], inner[1]))
    outer.append(move(owed, pairs))
    inner.append(move(sent, middle))
    return [(outer[4 + part], inner[2 + part]) for part in range(2)], beside


def per_device(
    n_dp, n, hidden_in, queries, keys_values, out_weight, send_rows, lengths, block_scales, value_head
):
    chunks = 2
    cols = hidden_in.shape[1] // chunks
    order = block_order(n, chunks)
    packed = pack_qkv(send_rows, queries, keys_values, n_dp)
    *packed, hidden_in = together(*packed, hidden_in)
    moved = exchange(packed, "dp", n_dp)
    packed_hidden, w_early = pack_hidden(
        send_rows, hidden_in, out_weight, n_dp, order, cols, 1 if n == 4 else 0
    )
    hidden = exchange(packed_hidden, "dp", n_dp)
    if n == 4:
        context, first = attend(lengths, moved, w_early[0])
        rest = project(context, out_weight, order, 1, cols, chunks)
        terms, own = [first, *rest[:-chunks]], rest[-chunks:]
        recv, hidden[1:] = chain_scatter(terms, hidden[1:])
    else:
        context = attend(lengths, moved)[0]
        partial_term = jnp.dot(context, out_weight, preferred_element_type=F32).astype(BF16)
        summed = lax.psum_scatter(partial_term, "tensor", scatter_dimension=1, tiled=True)
        zero = jnp.zeros((hidden_in.shape[0], cols), BF16)
        recv = [(summed[:, part * cols : (part + 1) * cols], zero) for part in range(chunks)]
        own = [zero] * chunks
    head_row = value_head.reshape(1, D)
    restored = sums = None
    for part in range(chunks):
        *rest, value, sums = finish(
            part, *recv[part], own[part], block_scales, head_row, hidden, sums, restored
        )
        restored = store(part, chunks, value, rest[0] if rest else None)
    sums = total_over(sums, "tensor", n)
    values = sums[1] / jnp.sqrt(sums[0] / D + EPS)
    return restored, values


def solution(mesh):
    in_specs = (
        P(("groups", "dp"), "tensor"),
        P(("groups", "dp"), "tensor"),
        P(("groups", "dp"), None, None),
        P("tensor", None),
        P(("groups", "dp"), None),
        P(("groups", "dp"), None),
        P(("groups", "dp"), "tensor"),
        P(),
    )
    out_specs = (P(("groups", "dp"), "tensor"), P(("groups", "dp")))
    return jax.shard_map(
        functools.partial(per_device, mesh.shape["dp"], mesh.shape["tensor"]),
        mesh=mesh,
        in_specs=in_specs,
        out_specs=out_specs,
        check_vma=False,
    )
```

```python
import functools

import jax
import jax.numpy as jnp
from jax import lax
from jax.experimental import pallas as pl
from jax.experimental.pallas import tpu as pltpu
from jax.sharding import PartitionSpec as P

D = 8192
HEADS = 32
KV_HEADS = 4
HD = 128
BLOCK = 128
GROUP = HEADS // KV_HEADS

CLIP_CODE = 448.0
EPS = 1e-06
F32 = jnp.float32
BF16 = jnp.bfloat16
VMEM = pl.BlockSpec(memory_space=pltpu.VMEM)
SMEM = pl.BlockSpec(memory_space=pltpu.SMEM)
ANY = pl.BlockSpec(memory_space=pl.ANY)
HBM = pl.BlockSpec(memory_space=pltpu.HBM)


def near(shape, dtype=BF16):
    return pltpu.VMEM(shape, dtype)


def held(value):
    return pltpu.with_memory_space_constraint(value, pltpu.VMEM)


def far(value):
    return pltpu.with_memory_space_constraint(value, pltpu.HBM)


def together(*values):
    return lax.optimization_barrier(values)


def params(mib):
    return pltpu.CompilerParams(vmem_limit_bytes=mib << 20)


def one_hot_columns(send_ref):
    rows = send_ref.shape[1]
    row_id = lax.broadcasted_iota(jnp.int32, (rows, rows), 0)
    return (row_id == send_ref[...]).astype(F32).astype(BF16)


def reorder(one_hot, values):
    return lax.dot_general(
        one_hot, values, (((0,), (0,)), ((), ())), preferred_element_type=F32
    ).astype(BF16)


def pack_qkv_kernel(heads_here, send_ref, q_ref, kv_ref, *refs):
    outs, buf = refs[:-1], refs[-1]
    me = lax.axis_index("dp")
    kv_head = lax.axis_index("tensor") * heads_here // GROUP
    one_hot = one_hot_columns(send_ref)
    width = q_ref.shape[1]
    buf[:, :width] = reorder(one_hot, q_ref[...])
    for pair in range(2):
        start = pl.multiple_of(kv_head * HD, HD)
        part = kv_ref[:, pair, pl.ds(start, HD)]
        buf[:, width + pair * HD : width + (pair + 1) * HD] = reorder(one_hot, part)
    share = outs[0].shape[0]
    for k, out in enumerate(outs):
        start = pl.multiple_of((me ^ k) * share, share)
        out[...] = buf[pl.ds(start, share), :]


def pack_qkv(send_rows, queries, keys_values, n_dp):
    rows, width = queries.shape
    out = near((rows // n_dp, width + 2 * HD))
    return pl.pallas_call(
        functools.partial(pack_qkv_kernel, width // HD),
        out_shape=[out] * n_dp,
        in_specs=[VMEM] * 3,
        out_specs=[VMEM] * n_dp,
        scratch_shapes=[pltpu.VMEM((rows, width + 2 * HD), BF16)],
        compiler_params=params(8),
        name="pack_qkv",
    )(far(send_rows), far(queries), far(keys_values))


FETCHES = 4


class Fetch:
    def __init__(self, order, place, w_ref, out, sems):
        depth, width = out.shape
        start = pl.multiple_of(order(place) * width, width)
        share = depth // FETCHES
        self.copies = []
        for k in range(FETCHES):
            rows = pl.ds(k * share, share)
            self.copies.append(
                pltpu.make_async_copy(w_ref.at[rows, pl.ds(start, width)], out.at[rows, :], sems.at[k])
            )
            self.copies[-1].start()

    def wait(self):
        for copy in self.copies:
            copy.wait()


def fetch_sems(blocks):
    return pltpu.SemaphoreType.DMA((max(blocks, 1), FETCHES))


def pack_hidden_kernel(n_dp, order, send_ref, h_ref, w_ref, *refs):
    outs, blocks, (buf, sems) = refs[:n_dp], refs[n_dp:-2], refs[-2:]
    copies = [Fetch(order, k, w_ref, block, sems.at[k]) for k, block in enumerate(blocks)]
    me = lax.axis_index("dp")
    buf[...] = reorder(one_hot_columns(send_ref), h_ref[...])
    share = outs[0].shape[0]
    for k, out in enumerate(outs):
        start = pl.multiple_of((me ^ k) * share, share)
        out[...] = buf[pl.ds(start, share), :]
    for copy in copies:
        copy.wait()


def pack_hidden(send_rows, hidden, weight, n_dp, order, cols, blocks):
    rows, width = hidden.shape
    depth = weight.shape[0]
    got = pl.pallas_call(
        functools.partial(pack_hidden_kernel, n_dp, order),
        out_shape=[near((rows // n_dp, width))] * n_dp + [near((depth, cols))] * blocks,
        in_specs=[VMEM] * 2 + [HBM],
        out_specs=[VMEM] * (n_dp + blocks),
        scratch_shapes=[pltpu.VMEM((rows, width), BF16), fetch_sems(blocks)],
        compiler_params=params(4 + 2 * blocks),
        name="pack_hidden",
    )(far(send_rows), far(hidden), far(weight))
    return got[:n_dp], got[n_dp:]


def attention(len_ref, pieces, buf, width):
    n_dp = len(pieces)
    rows = buf.shape[0]
    me = lax.axis_index("dp")
    share = pieces[0].shape[0]
    for k, piece in zip(arrivals(n_dp), pieces):
        start = pl.multiple_of((me ^ k) * share, share)
        buf[pl.ds(start, share), :] = piece[...]
    row_id = lax.broadcasted_iota(jnp.int32, (rows, rows), 0)
    col_id = lax.broadcasted_iota(jnp.int32, (rows, rows), 1)
    row_seg = jnp.zeros((rows, rows), jnp.int32)
    col_seg = jnp.zeros((rows, rows), jnp.int32)
    end = jnp.int32(0)
    for r in range(len_ref.shape[1]):
        end = end + len_ref[0, r]
        row_seg += (row_id >= end).astype(jnp.int32)
        col_seg += (col_id >= end).astype(jnp.int32)
    allowed = (row_seg == col_seg) & (row_id >= col_id)
    heads = width // HD
    keys = buf[:, width : width + HD]
    values = jnp.concatenate(
        [buf[:, width + HD : width + 2 * HD], jnp.ones((rows, HD), BF16)], axis=1
    )
    query = jnp.concatenate([buf[:, h * HD : (h + 1) * HD] for h in range(heads)], axis=0)
    scores = lax.dot_general(
        query, keys, (((1,), (1,)), ((), ())), preferred_element_type=F32
    ) * HD ** (-0.5)
    scores = jnp.where(allowed[None], scores.reshape(heads, rows, rows), -jnp.inf)
    weights = jnp.exp(scores - jnp.max(scores, axis=2, keepdims=True))
    weights = weights.reshape(heads * rows, rows).astype(BF16)
    mixed = jnp.dot(weights, values, preferred_element_type=F32)
    context = (mixed[:, :HD] / mixed[:, HD:]).astype(BF16)
    return jnp.concatenate([context[h * rows : (h + 1) * rows] for h in range(heads)], axis=1)


def attend_kernel(len_ref, *refs):
    pieces, out, buf = refs[:-2], refs[-2], refs[-1]
    out[...] = attention(len_ref, pieces, buf, out.shape[1])


def at_an_end():
    i = lax.axis_index("tensor")
    return (i == 0) | (i == 3)


def first_kernel(len_ref, *refs):
    pieces, (w_ref, out, first, buf) = refs[:-4], refs[-4:]

    @pl.when(at_an_end())
    def _():
        context = attention(len_ref, pieces, buf, out.shape[1])
        out[...] = context
        first[...] = jnp.dot(context, w_ref[...], preferred_element_type=F32).astype(BF16)


def arrivals(n_dp):
    return [0, 2, 1, *range(3, n_dp)] if n_dp > 2 else [*range(n_dp)]


def arrived(pieces):
    return [held(pieces[k]) for k in arrivals(len(pieces))]


def attend(lengths, pieces):
    share, wide = pieces[0].shape
    rows, width = share * len(pieces), wide - 2 * HD
    return pl.pallas_call(
        attend_kernel,
        out_shape=near((rows, width)),
        in_specs=[SMEM] + [VMEM] * len(pieces),
        out_specs=VMEM,
        scratch_shapes=[pltpu.VMEM((rows, wide), BF16)],
        compiler_params=params(8),
        name="attend",
    )(lengths, *arrived(pieces))


def attend_first(lengths, pieces, block):
    share, wide = pieces[0].shape
    rows, width = share * len(pieces), wide - 2 * HD
    return pl.pallas_call(
        first_kernel,
        out_shape=[near((rows, width)), near((rows, block.shape[1]))],
        in_specs=[SMEM] + [VMEM] * (len(pieces) + 1),
        out_specs=[VMEM] * 2,
        scratch_shapes=[pltpu.VMEM((rows, wide), BF16)],
        compiler_params=params(8),
        name="attend_first",
    )(lengths, *arrived(pieces), held(block))


def project_kernel(n_dp, order, len_ref, ctx_ref, w_ref, *refs):
    pieces, outs, (context, buf) = refs[:n_dp], refs[n_dp:-2], refs[-2:]
    end = at_an_end()

    @pl.when(end)
    def _():
        context[...] = ctx_ref[...]

    @pl.when(jnp.logical_not(end))
    def _():
        context[...] = attention(len_ref, pieces, buf, context.shape[1])

    for k, out in enumerate(outs):
        width = out.shape[1]
        start = pl.multiple_of(order(k) * width, width)
        term = jnp.dot(context[...], w_ref[:, pl.ds(start, width)], preferred_element_type=F32)
        out[...] = term.astype(out.dtype)


def project(lengths, pieces, context, weight, order, cols, kept):
    rows, depth = context.shape
    wide = pieces[0].shape[1]
    count = weight.shape[1] // cols
    return pl.pallas_call(
        functools.partial(project_kernel, len(pieces), order),
        out_shape=[
            near((rows, cols), F32 if place >= count - kept else BF16) for place in range(count)
        ],
        in_specs=[SMEM] + [VMEM] * (2 + len(pieces)),
        out_specs=[VMEM] * count,
        scratch_shapes=[pltpu.VMEM((rows, depth), BF16), pltpu.VMEM((rows, wide), BF16)],
        compiler_params=params(8),
        cost_estimate=pl.CostEstimate(
            flops=2 * rows * depth * cols * count,
            bytes_accessed=2 * depth * cols * count,
            transcendentals=0,
        ),
        name="project",
    )(lengths, held(context), held(weight), *arrived(pieces))


def add_kernel(count, *refs):
    for a_ref, b_ref, out in zip(refs[:count], refs[count : 2 * count], refs[-count:]):
        out[...] = (a_ref[...].astype(F32) + b_ref[...].astype(F32)).astype(BF16)


def add(*pairs, after=()):
    count = len(pairs)
    left, right = zip(*pairs)
    return pl.pallas_call(
        functools.partial(add_kernel, count),
        out_shape=[near(a.shape) for a in (*after, *left)],
        in_specs=[VMEM] * (2 * count) + [ANY] * len(after),
        out_specs=[ANY] * len(after) + [VMEM] * count,
        input_output_aliases={2 * count + k: k for k in range(len(after))},
        compiler_params=params(4),
        name="add",
    )(*map(held, left), *map(held, right), *map(held, after))


def finish_kernel(n_dp, part, width, recv_r, recv_l, own, scale_ref, head_ref, *refs):
    pieces = refs[:n_dp]
    out, sums = refs[-2:]
    earlier = refs[n_dp] if part else None
    me = lax.axis_index("dp")
    i = lax.axis_index("tensor")
    share = pieces[0].shape[0]
    rows, cols = recv_r.shape
    base = part * cols
    for k, piece in enumerate(pieces):
        start = pl.multiple_of((me ^ k) * share, share)
        out[pl.ds(start, share), :] = piece[:, base : base + cols].astype(F32)
    power = jnp.zeros((rows, BLOCK), F32)
    dots = jnp.zeros((rows, BLOCK), F32)
    for b in range(cols // BLOCK):
        here = slice(b * BLOCK, (b + 1) * BLOCK)
        block = base // BLOCK + b
        scale = scale_ref[:, block : block + 1].astype(F32)
        summed = recv_r[:, here].astype(F32) + recv_l[:, here].astype(F32) + own[:, here]
        residual = out[:, here] + summed
        code = jnp.clip(residual / scale, -CLIP_CODE, CLIP_CODE).astype(BF16)
        restored = code.astype(F32) * scale
        out[:, here] = restored
        power += restored * restored
        start = pl.multiple_of(i * width + base + b * BLOCK, BLOCK)
        dots += restored * head_ref[:, pl.ds(start, BLOCK)].astype(F32)
    total = jnp.concatenate(
        [
            jnp.sum(jnp.transpose(power), axis=0, keepdims=True),
            jnp.sum(jnp.transpose(dots), axis=0, keepdims=True),
            jnp.zeros((6, rows), F32),
        ],
        axis=0,
    )
    if part:
        total = total + earlier[...]
    sums[...] = total


def finish(part, recv_r, recv_l, own, scales, head_row, pieces, earlier=None, stored=None):
    rows, cols = recv_r.shape
    width = pieces[0].shape[1]
    n_dp = len(pieces)
    args = [*map(held, (recv_r, recv_l, own)), scales, head_row, *map(held, pieces)]
    outs = [near((rows, cols), F32), near((8, rows), F32)]
    if part:
        args += [held(earlier), far(stored)]
        outs = [jax.ShapeDtypeStruct(stored.shape, F32), *outs]
    return pl.pallas_call(
        functools.partial(finish_kernel, n_dp, part, width),
        out_shape=outs,
        in_specs=[VMEM] * (len(args) - 1) + [ANY if part else VMEM],
        out_specs=[ANY] * (len(outs) - 2) + [VMEM] * 2,
        input_output_aliases={len(args) - 1: 0} if part else {},
        compiler_params=params(8),
        name="finish",
    )(*args)


def store_kernel(part, value_ref, *refs):
    out, sem = refs[-2:]
    cols = value_ref.shape[1]
    copy = pltpu.make_async_copy(value_ref, out.at[:, pl.ds(part * cols, cols)], sem)
    copy.start()
    copy.wait()


def store(part, chunks, value, before):
    rows, cols = value.shape
    args = [held(value)] + ([] if before is None else [before])
    return pl.pallas_call(
        functools.partial(store_kernel, part),
        out_shape=jax.ShapeDtypeStruct((rows, cols * chunks), F32),
        in_specs=[VMEM] + [ANY] * (len(args) - 1),
        out_specs=ANY,
        input_output_aliases={1: 0} if len(args) > 1 else {},
        scratch_shapes=[pltpu.SemaphoreType.DMA],
        compiler_params=params(4),
        cost_estimate=pl.CostEstimate(
            flops=0, bytes_accessed=4 * rows * cols, transcendentals=0
        ),
        name="store",
    )(*args)


def swap(piece, axis, n, bits):
    return lax.ppermute(piece, axis, [(i, i ^ bits) for i in range(n)])


def exchange(pieces, axis, n):
    return [pieces[0]] + [swap(pieces[k], axis, n, k) for k in range(1, n)]


def total_over(values, axis, n):
    done = 1
    while done < n:
        radix = min(4, n // done)
        got = [values] + [swap(values, axis, n, k * done) for k in range(1, radix)]
        values = got[0] + got[1] if radix == 2 else (got[2] + got[0]) + (got[1] + got[3])
        done *= radix
    return values


def block_order(n, chunks):
    def order(place):
        turn, part = place // chunks, place % chunks
        i = lax.axis_index("tensor")
        low = i < 2
        away = jnp.where(low, 3 - turn, turn)
        if turn < 2:
            shard = away
        elif turn == 2:
            shard = jnp.where(i == 0, 1, jnp.where(i == 1, 0, jnp.where(i == 2, 3, 2)))
        else:
            shard = i
        return shard * chunks + part

    return order if n == 4 else lambda place: jnp.int32(place)


def chain_scatter(first, terms, beside):
    ends = [(0, 1), (3, 2)]
    pairs = [(0, 1), (1, 0), (2, 3), (3, 2)]
    middle = [(1, 2), (2, 1)]
    move = lambda value, perm: lax.ppermute(value, "tensor", perm)
    t = list(terms)
    outer = [move(first, ends), move(t[1], ends)]
    t[2], t[3], sent = add((t[0], outer[0]), after=[t[2], t[3]])
    outer.append(move(t[2], ends))
    inner = [move(sent, middle)]
    t[3], t[4], *beside, sent = add((t[1], outer[1]), after=[t[3], t[4], *beside])
    outer.append(move(t[3], ends))
    inner.append(move(sent, middle))
    t[5], sent, owed = add((t[2], outer[2]), (t[4], inner[0]), after=[t[5]])
    outer.append(move(owed, pairs))
    inner.append(move(sent, middle))
    sent, owed = add((t[3], outer[3]), (t[5], inner[1]))
    outer.append(move(owed, pairs))
    inner.append(move(sent, middle))
    return [(outer[4 + part], inner[2 + part]) for part in range(2)], beside


def per_device(
    n_dp, n, hidden_in, queries, keys_values, out_weight, send_rows, lengths, block_scales, value_head
):
    chunks = 2
    cols = hidden_in.shape[1] // chunks
    order = block_order(n, chunks)
    packed = pack_qkv(send_rows, queries, keys_values, n_dp)
    *packed, hidden_in = together(*packed, hidden_in)
    moved = exchange(packed, "dp", n_dp)
    packed_hidden, w_early = pack_hidden(
        send_rows, hidden_in, out_weight, n_dp, order, cols, 1 if n == 4 else 0
    )
    hidden = exchange(packed_hidden, "dp", n_dp)
    if n == 4:
        context, first = attend_first(lengths, moved, w_early[0])
        blocks = project(lengths, moved, context, out_weight, order, cols, chunks)
        terms, own = blocks[:-chunks], blocks[-chunks:]
        recv, hidden[1:] = chain_scatter(first, terms, hidden[1:])
    else:
        context = attend(lengths, moved)
        partial_term = jnp.dot(context, out_weight, preferred_element_type=F32).astype(BF16)
        summed = lax.psum_scatter(partial_term, "tensor", scatter_dimension=1, tiled=True)
        zero = jnp.zeros((hidden_in.shape[0], cols), BF16)
        recv = [(summed[:, part * cols : (part + 1) * cols], zero) for part in range(chunks)]
        own = [zero] * chunks
    head_row = value_head.reshape(1, D)
    restored = sums = None
    for part in range(chunks):
        *rest, value, sums = finish(
            part, *recv[part], own[part], block_scales, head_row, hidden, sums, restored
        )
        restored = store(part, chunks, value, rest[0] if rest else None)
    sums = total_over(sums, "tensor", n)
    values = sums[1] / jnp.sqrt(sums[0] / D + EPS)
    return restored, values


def solution(mesh):
    in_specs = (
        P(("groups", "dp"), "tensor"),
        P(("groups", "dp"), "tensor"),
        P(("groups", "dp"), None, None),
        P("tensor", None),
        P(("groups", "dp"), None),
        P(("groups", "dp"), None),
        P(("groups", "dp"), "tensor"),
        P(),
    )
    out_specs = (P(("groups", "dp"), "tensor"), P(("groups", "dp")))
    return jax.shard_map(
        functools.partial(per_device, mesh.shape["dp"], mesh.shape["tensor"]),
        mesh=mesh,
        in_specs=in_specs,
        out_specs=out_specs,
        check_vma=False,
    )
```

```python
import functools

import jax
import jax.numpy as jnp
from jax import lax
from jax.experimental import pallas as pl
from jax.experimental.pallas import tpu as pltpu
from jax.sharding import PartitionSpec as P

D = 8192
HEADS = 32
KV_HEADS = 4
HD = 128
BLOCK = 128
GROUP = HEADS // KV_HEADS

CLIP_CODE = 448.0
EPS = 1e-06
F32 = jnp.float32
BF16 = jnp.bfloat16
VMEM = pl.BlockSpec(memory_space=pltpu.VMEM)
SMEM = pl.BlockSpec(memory_space=pltpu.SMEM)
ANY = pl.BlockSpec(memory_space=pl.ANY)
HBM = pl.BlockSpec(memory_space=pltpu.HBM)


def near(shape, dtype=BF16):
    return pltpu.VMEM(shape, dtype)


def held(value):
    return pltpu.with_memory_space_constraint(value, pltpu.VMEM)


def far(value):
    return pltpu.with_memory_space_constraint(value, pltpu.HBM)


def together(*values):
    return lax.optimization_barrier(values)


def params(mib):
    return pltpu.CompilerParams(vmem_limit_bytes=mib << 20)


def one_hot_columns(send_ref):
    rows = send_ref.shape[1]
    row_id = lax.broadcasted_iota(jnp.int32, (rows, rows), 0)
    return (row_id == send_ref[...]).astype(F32).astype(BF16)


def reorder(one_hot, values):
    return lax.dot_general(
        one_hot, values, (((0,), (0,)), ((), ())), preferred_element_type=F32
    ).astype(BF16)


def pack_qkv_kernel(heads_here, send_ref, q_ref, kv_ref, *refs):
    outs, buf = refs[:-1], refs[-1]
    me = lax.axis_index("dp")
    kv_head = lax.axis_index("tensor") * heads_here // GROUP
    one_hot = one_hot_columns(send_ref)
    width = q_ref.shape[1]
    buf[:, :width] = reorder(one_hot, q_ref[...])
    for pair in range(2):
        start = pl.multiple_of(kv_head * HD, HD)
        part = kv_ref[:, pair, pl.ds(start, HD)]
        buf[:, width + pair * HD : width + (pair + 1) * HD] = reorder(one_hot, part)
    share = outs[0].shape[0]
    for k, out in enumerate(outs):
        start = pl.multiple_of((me ^ k) * share, share)
        out[...] = buf[pl.ds(start, share), :]


def pack_qkv(send_rows, queries, keys_values, n_dp):
    rows, width = queries.shape
    out = near((rows // n_dp, width + 2 * HD))
    return pl.pallas_call(
        functools.partial(pack_qkv_kernel, width // HD),
        out_shape=[out] * n_dp,
        in_specs=[VMEM] * 3,
        out_specs=[VMEM] * n_dp,
        scratch_shapes=[pltpu.VMEM((rows, width + 2 * HD), BF16)],
        compiler_params=params(8),
        name="pack_qkv",
    )(far(send_rows), far(queries), far(keys_values))


FETCHES = 4


class Fetch:
    def __init__(self, order, place, w_ref, out, sems):
        depth, width = out.shape
        start = pl.multiple_of(order(place) * width, width)
        share = depth // FETCHES
        self.copies = []
        for k in range(FETCHES):
            rows = pl.ds(k * share, share)
            self.copies.append(
                pltpu.make_async_copy(w_ref.at[rows, pl.ds(start, width)], out.at[rows, :], sems.at[k])
            )

    def start(self):
        for copy in self.copies:
            copy.start()

    def wait(self):
        for copy in self.copies:
            copy.wait()


def allowed_pairs(len_ref, rows):
    row_id = lax.broadcasted_iota(jnp.int32, (rows, rows), 0)
    col_id = lax.broadcasted_iota(jnp.int32, (rows, rows), 1)
    row_seg = jnp.zeros((rows, rows), jnp.int32)
    col_seg = jnp.zeros((rows, rows), jnp.int32)
    end = jnp.int32(0)
    for r in range(len_ref.shape[1]):
        end = end + len_ref[0, r]
        row_seg += (row_id >= end).astype(jnp.int32)
        col_seg += (col_id >= end).astype(jnp.int32)
    return (row_seg == col_seg) & (row_id >= col_id)


def pack_hidden_kernel(n_dp, order, len_ref, send_ref, h_ref, w_ref, *refs):
    outs, mask_out, (buf, sems) = refs[:n_dp], refs[n_dp], refs[-2:]
    block = refs[n_dp + 1] if len(refs) > n_dp + 3 else None
    if block is not None:

        @pl.when(at_an_end())
        def _():
            Fetch(order, 0, w_ref, block, sems).start()

    mask_out[...] = allowed_pairs(len_ref, mask_out.shape[0]).astype(F32)
    me = lax.axis_index("dp")
    buf[...] = reorder(one_hot_columns(send_ref), h_ref[...])
    share = outs[0].shape[0]
    for k, out in enumerate(outs):
        start = pl.multiple_of((me ^ k) * share, share)
        out[...] = buf[pl.ds(start, share), :]
    if block is not None:

        @pl.when(at_an_end())
        def _():
            Fetch(order, 0, w_ref, block, sems).wait()


def pack_hidden(lengths, send_rows, hidden, weight, n_dp, order, cols, blocks):
    rows, width = hidden.shape
    depth = weight.shape[0]
    got = pl.pallas_call(
        functools.partial(pack_hidden_kernel, n_dp, order),
        out_shape=[near((rows // n_dp, width))] * n_dp
        + [near((rows, rows), F32)]
        + [near((depth, cols))] * blocks,
        in_specs=[SMEM] + [VMEM] * 2 + [HBM],
        out_specs=[VMEM] * (n_dp + 1 + blocks),
        scratch_shapes=[pltpu.VMEM((rows, width), BF16), pltpu.SemaphoreType.DMA((FETCHES,))],
        compiler_params=params(4 + 2 * blocks),
        name="pack_hidden",
    )(far(lengths), far(send_rows), far(hidden), far(weight))
    return got[:n_dp], got[n_dp], got[n_dp + 1 :]


def attention(mask_ref, pieces, buf, width):
    n_dp = len(pieces)
    rows = buf.shape[0]
    me = lax.axis_index("dp")
    share = pieces[0].shape[0]
    for k, piece in zip(arrivals(n_dp), pieces):
        start = pl.multiple_of((me ^ k) * share, share)
        buf[pl.ds(start, share), :] = piece[...]
    heads = width // HD
    keys = buf[:, width : width + HD]
    values = jnp.concatenate(
        [buf[:, width + HD : width + 2 * HD], jnp.ones((rows, HD), BF16)], axis=1
    )
    query = jnp.concatenate([buf[:, h * HD : (h + 1) * HD] for h in range(heads)], axis=0)
    scores = lax.dot_general(
        query, keys, (((1,), (1,)), ((), ())), preferred_element_type=F32
    ) * HD ** (-0.5)
    scores = jnp.where(mask_ref[...][None] > 0, scores.reshape(heads, rows, rows), -jnp.inf)
    weights = jnp.exp(scores - jnp.max(scores, axis=2, keepdims=True))
    weights = weights.reshape(heads * rows, rows).astype(BF16)
    mixed = jnp.dot(weights, values, preferred_element_type=F32)
    context = (mixed[:, :HD] / mixed[:, HD:]).astype(BF16)
    return jnp.concatenate([context[h * rows : (h + 1) * rows] for h in range(heads)], axis=1)


def attend_kernel(mask_ref, *refs):
    pieces, out, buf = refs[:-2], refs[-2], refs[-1]
    out[...] = attention(mask_ref, pieces, buf, out.shape[1])


def at_an_end():
    i = lax.axis_index("tensor")
    return (i == 0) | (i == 3)


def first_kernel(mask_ref, *refs):
    pieces, (w_ref, out, first, buf) = refs[:-4], refs[-4:]

    @pl.when(at_an_end())
    def _():
        context = attention(mask_ref, pieces, buf, out.shape[1])
        out[...] = context
        first[...] = jnp.dot(context, w_ref[...], preferred_element_type=F32).astype(BF16)


def arrivals(n_dp):
    return [0, 2, 1, *range(3, n_dp)] if n_dp > 2 else [*range(n_dp)]


def arrived(pieces):
    return [held(pieces[k]) for k in arrivals(len(pieces))]


def attend(mask, pieces):
    share, wide = pieces[0].shape
    rows, width = share * len(pieces), wide - 2 * HD
    return pl.pallas_call(
        attend_kernel,
        out_shape=near((rows, width)),
        in_specs=[VMEM] * (1 + len(pieces)),
        out_specs=VMEM,
        scratch_shapes=[pltpu.VMEM((rows, wide), BF16)],
        compiler_params=params(8),
        name="attend",
    )(held(mask), *arrived(pieces))


def attend_first(mask, pieces, block):
    share, wide = pieces[0].shape
    rows, width = share * len(pieces), wide - 2 * HD
    return pl.pallas_call(
        first_kernel,
        out_shape=[near((rows, width)), near((rows, block.shape[1]))],
        in_specs=[VMEM] * (len(pieces) + 2),
        out_specs=[VMEM] * 2,
        scratch_shapes=[pltpu.VMEM((rows, wide), BF16)],
        compiler_params=params(8),
        name="attend_first",
    )(held(mask), *arrived(pieces), held(block))


def project_kernel(n_dp, order, mask_ref, ctx_ref, w_ref, *refs):
    pieces, outs, (context, buf) = refs[:n_dp], refs[n_dp:-2], refs[-2:]
    end = at_an_end()

    @pl.when(end)
    def _():
        context[...] = ctx_ref[...]

    @pl.when(jnp.logical_not(end))
    def _():
        context[...] = attention(mask_ref, pieces, buf, context.shape[1])

    for k, out in enumerate(outs):
        width = out.shape[1]
        start = pl.multiple_of(order(k) * width, width)
        term = jnp.dot(context[...], w_ref[:, pl.ds(start, width)], preferred_element_type=F32)
        out[...] = term.astype(out.dtype)


def project(mask, pieces, context, weight, order, cols, kept):
    rows, depth = context.shape
    wide = pieces[0].shape[1]
    count = weight.shape[1] // cols
    return pl.pallas_call(
        functools.partial(project_kernel, len(pieces), order),
        out_shape=[
            near((rows, cols), F32 if place >= count - kept else BF16) for place in range(count)
        ],
        in_specs=[VMEM] * (3 + len(pieces)),
        out_specs=[VMEM] * count,
        scratch_shapes=[pltpu.VMEM((rows, depth), BF16), pltpu.VMEM((rows, wide), BF16)],
        compiler_params=params(8),
        cost_estimate=pl.CostEstimate(
            flops=2 * rows * depth * cols * count,
            bytes_accessed=2 * depth * cols * count,
            transcendentals=0,
        ),
        name="project",
    )(held(mask), held(context), held(weight), *arrived(pieces))


def add_kernel(count, *refs):
    for a_ref, b_ref, out in zip(refs[:count], refs[count : 2 * count], refs[-count:]):
        out[...] = (a_ref[...].astype(F32) + b_ref[...].astype(F32)).astype(BF16)


def add(*pairs, after=()):
    count = len(pairs)
    left, right = zip(*pairs)
    return pl.pallas_call(
        functools.partial(add_kernel, count),
        out_shape=[near(a.shape) for a in (*after, *left)],
        in_specs=[VMEM] * (2 * count) + [ANY] * len(after),
        out_specs=[ANY] * len(after) + [VMEM] * count,
        input_output_aliases={2 * count + k: k for k in range(len(after))},
        compiler_params=params(4),
        name="add",
    )(*map(held, left), *map(held, right), *map(held, after))


def finish_kernel(n_dp, part, width, recv_r, recv_l, own, scale_ref, head_ref, *refs):
    pieces = refs[:n_dp]
    out, sums = refs[-2:]
    earlier = refs[n_dp] if part else None
    me = lax.axis_index("dp")
    i = lax.axis_index("tensor")
    share = pieces[0].shape[0]
    rows, cols = recv_r.shape
    base = part * cols
    for k, piece in enumerate(pieces):
        start = pl.multiple_of((me ^ k) * share, share)
        out[pl.ds(start, share), :] = piece[:, base : base + cols].astype(F32)
    power = jnp.zeros((rows, BLOCK), F32)
    dots = jnp.zeros((rows, BLOCK), F32)
    for b in range(cols // BLOCK):
        here = slice(b * BLOCK, (b + 1) * BLOCK)
        block = base // BLOCK + b
        scale = scale_ref[:, block : block + 1].astype(F32)
        summed = recv_r[:, here].astype(F32) + recv_l[:, here].astype(F32) + own[:, here]
        residual = out[:, here] + summed
        code = jnp.clip(residual / scale, -CLIP_CODE, CLIP_CODE).astype(BF16)
        restored = code.astype(F32) * scale
        out[:, here] = restored
        power += restored * restored
        start = pl.multiple_of(i * width + base + b * BLOCK, BLOCK)
        dots += restored * head_ref[:, pl.ds(start, BLOCK)].astype(F32)
    total = jnp.concatenate(
        [
            jnp.sum(jnp.transpose(power), axis=0, keepdims=True),
            jnp.sum(jnp.transpose(dots), axis=0, keepdims=True),
            jnp.zeros((6, rows), F32),
        ],
        axis=0,
    )
    if part:
        total = total + earlier[...]
    sums[...] = total


def finish(part, recv_r, recv_l, own, scales, head_row, pieces, earlier=None, stored=None):
    rows, cols = recv_r.shape
    width = pieces[0].shape[1]
    n_dp = len(pieces)
    args = [*map(held, (recv_r, recv_l, own)), scales, head_row, *map(held, pieces)]
    outs = [near((rows, cols), F32), near((8, rows), F32)]
    if part:
        args += [held(earlier), far(stored)]
        outs = [jax.ShapeDtypeStruct(stored.shape, F32), *outs]
    return pl.pallas_call(
        functools.partial(finish_kernel, n_dp, part, width),
        out_shape=outs,
        in_specs=[VMEM] * (len(args) - 1) + [ANY if part else VMEM],
        out_specs=[ANY] * (len(outs) - 2) + [VMEM] * 2,
        input_output_aliases={len(args) - 1: 0} if part else {},
        compiler_params=params(8),
        name="finish",
    )(*args)


def store_kernel(part, value_ref, *refs):
    out, sem = refs[-2:]
    cols = value_ref.shape[1]
    copy = pltpu.make_async_copy(value_ref, out.at[:, pl.ds(part * cols, cols)], sem)
    copy.start()
    copy.wait()


def store(part, chunks, value, before):
    rows, cols = value.shape
    args = [held(value)] + ([] if before is None else [before])
    return pl.pallas_call(
        functools.partial(store_kernel, part),
        out_shape=jax.ShapeDtypeStruct((rows, cols * chunks), F32),
        in_specs=[VMEM] + [ANY] * (len(args) - 1),
        out_specs=ANY,
        input_output_aliases={1: 0} if len(args) > 1 else {},
        scratch_shapes=[pltpu.SemaphoreType.DMA],
        compiler_params=params(4),
        cost_estimate=pl.CostEstimate(
            flops=0, bytes_accessed=4 * rows * cols, transcendentals=0
        ),
        name="store",
    )(*args)


def swap(piece, axis, n, bits):
    return lax.ppermute(piece, axis, [(i, i ^ bits) for i in range(n)])


def exchange(pieces, axis, n):
    return [pieces[0]] + [swap(pieces[k], axis, n, k) for k in range(1, n)]


def total_over(values, axis, n):
    done = 1
    while done < n:
        radix = min(4, n // done)
        got = [values] + [swap(values, axis, n, k * done) for k in range(1, radix)]
        values = got[0] + got[1] if radix == 2 else (got[3] + got[0]) + (got[2] + got[1])
        done *= radix
    return values


def block_order(n, chunks):
    def order(place):
        turn, part = place // chunks, place % chunks
        i = lax.axis_index("tensor")
        low = i < 2
        away = jnp.where(low, 3 - turn, turn)
        if turn < 2:
            shard = away
        elif turn == 2:
            shard = jnp.where(i == 0, 1, jnp.where(i == 1, 0, jnp.where(i == 2, 3, 2)))
        else:
            shard = i
        return shard * chunks + part

    return order if n == 4 else lambda place: jnp.int32(place)


def chain_scatter(first, terms, beside):
    ends = [(0, 1), (3, 2)]
    pairs = [(0, 1), (1, 0), (2, 3), (3, 2)]
    middle = [(1, 2), (2, 1)]
    move = lambda value, perm: lax.ppermute(value, "tensor", perm)
    t = list(terms)
    outer = [move(first, ends), move(t[1], ends)]
    t[2], t[3], sent = add((t[0], outer[0]), after=[t[2], t[3]])
    outer.append(move(t[2], ends))
    inner = [move(sent, middle)]
    t[3], t[4], *beside, sent = add((t[1], outer[1]), after=[t[3], t[4], *beside])
    outer.append(move(t[3], ends))
    inner.append(move(sent, middle))
    t[5], sent, owed = add((t[2], outer[2]), (t[4], inner[0]), after=[t[5]])
    outer.append(move(owed, pairs))
    inner.append(move(sent, middle))
    sent, owed = add((t[3], outer[3]), (t[5], inner[1]))
    outer.append(move(owed, pairs))
    inner.append(move(sent, middle))
    return [(outer[4 + part], inner[2 + part]) for part in range(2)], beside


def per_device(
    n_dp, n, hidden_in, queries, keys_values, out_weight, send_rows, lengths, block_scales, value_head
):
    chunks = 2
    cols = hidden_in.shape[1] // chunks
    order = block_order(n, chunks)
    packed = pack_qkv(send_rows, queries, keys_values, n_dp)
    *packed, hidden_in = together(*packed, hidden_in)
    moved = exchange(packed, "dp", n_dp)
    packed_hidden, mask, w_early = pack_hidden(
        lengths, send_rows, hidden_in, out_weight, n_dp, order, cols, 1 if n == 4 else 0
    )
    hidden = exchange(packed_hidden, "dp", n_dp)
    if n == 4:
        context, first = attend_first(mask, moved, w_early[0])
        blocks = project(mask, moved, context, out_weight, order, cols, chunks)
        terms, own = blocks[:-chunks], blocks[-chunks:]
        recv, hidden[1:] = chain_scatter(first, terms, hidden[1:])
    else:
        context = attend(mask, moved)
        partial_term = jnp.dot(context, out_weight, preferred_element_type=F32).astype(BF16)
        summed = lax.psum_scatter(partial_term, "tensor", scatter_dimension=1, tiled=True)
        zero = jnp.zeros((hidden_in.shape[0], cols), BF16)
        recv = [(summed[:, part * cols : (part + 1) * cols], zero) for part in range(chunks)]
        own = [zero] * chunks
    head_row = value_head.reshape(1, D)
    restored = sums = None
    for part in range(chunks):
        *rest, value, sums = finish(
            part, *recv[part], own[part], block_scales, head_row, hidden, sums, restored
        )
        restored = store(part, chunks, value, rest[0] if rest else None)
    sums = total_over(sums, "tensor", n)
    values = sums[1] / jnp.sqrt(sums[0] / D + EPS)
    return restored, values


def solution(mesh):
    in_specs = (
        P(("groups", "dp"), "tensor"),
        P(("groups", "dp"), "tensor"),
        P(("groups", "dp"), None, None),
        P("tensor", None),
        P(("groups", "dp"), None),
        P(("groups", "dp"), None),
        P(("groups", "dp"), "tensor"),
        P(),
    )
    out_specs = (P(("groups", "dp"), "tensor"), P(("groups", "dp")))
    return jax.shard_map(
        functools.partial(per_device, mesh.shape["dp"], mesh.shape["tensor"]),
        mesh=mesh,
        in_specs=in_specs,
        out_specs=out_specs,
        check_vma=False,
    )
```
